512 devices in a mesh: hours: 64 (over z, x, core), region: 8 (over y).
Axes of the slice: x: 4, y: 8, z: 8, core: 2. Of those that a mesh axis runs over, the one named last changes fastest.
Arguments:
- availability: float32 [4096, 16, 1024], P('hours', None, 'region'), may hold values from 0.1 to 1
- demand: float32 [4096, 1024], P('hours', 'region'), may hold values from 2 to 72, as said below
- gen_cost: float32 [16, 1024], P(None, 'region'), may hold values from 0.05 to 1
- cap_cost: float32 [8, 2048], P('region', 'hours'), may hold values from 204.8 to 2048
- owner_map: int32 [8, 2048], P('region'), may hold values from 0 to 2047, each once within a row
- line_ends: int32 [2, 2048], P(None, 'region'), may hold values from 0 to 127
- line_limit: float32 [2048], P('region'), may hold values from 0.5 to 4
- cross_ends: int32 [2, 8, 256], P(None, 'region'), may hold values from 0 to 127
- cross_limit: float32 [8, 256], P('region'), may hold values from 0.5 to 4
- pair_counts: int32 [8, 8], P('region'), may hold values from 0 to 32, as said below
- store_node: int32 [2048], P('region'), may hold values from 0 to 127
- store_energy: float32 [2048], P('region'), may hold values from 0.02 to 0.4
- store_power: float32 [2048], P('region'), may hold values from 0.2 to 2
- price_start: float32 [4096, 1024], P('hours', 'region'), may hold values from -3 to 0.5
Outputs:
- dispatch: float32 [4096, 16, 1024], P('hours', None, 'region')
- capacity: float32 [8, 2048], P('region', 'hours')
- prices: float32 [4096, 1024], P('hours', 'region')
- charge_state: float32 [4096, 2048], P('hours', 'region')
The draws below stay inside these ranges and needn't reach their ends.
Inputs may be any that keep to these rules, and one draw needn't show every extreme that they name: `demand`: loads are positive. `owner_map`: each row lists every capacity column of its region once. `pair_counts`: cross lines in use among the 32 slots of each ordered pair of regions; a region has none to itself; some pair uses all 32.
All inputs are finite; a program needn't handle non-finite values.
Results may differ from the reference program's by a relative error of at most 0.00018.
Values sent between devices are 32-bit elements; how exact they have to be, the bound alone decides.
A program may use at most 64 MiB of HBM per device.

```python
import math
import jax
import jax.numpy as jnp
from jax import lax

K = 16
NODE_DEV = 128
LIN_DEV = 256
XW = 32
S_DEV = 256
ITERS = 4
HOURS = 4096
NODES = 1024
LINES = 2048
SLOTS = 256
STORES = 2048
COLS = 2048
N_REGION = 8


def draw_demand(key, part):
    first_key = jax.random.fold_in(jax.random.fold_in(key, 11), 0)
    hour_ramp = 1.0 + 2.0 * jnp.arange(HOURS, dtype=jnp.float32)[:, None] / (HOURS - 1)
    base_load = jax.random.uniform(first_key, (HOURS, NODES), jnp.float32, 4.0, 12.0)
    return (base_load * hour_ramp).astype(jnp.float32)


def draw_pair_counts(key, part):
    first_key, second_key = jax.random.split(jax.random.fold_in(key, 23))
    counts = jax.random.randint(first_key, (N_REGION, N_REGION), 1, XW + 1)
    chosen = jax.random.randint(second_key, (), 0, N_REGION * (N_REGION - 1))
    source = chosen // (N_REGION - 1)
    offset = chosen % (N_REGION - 1)
    target = offset + (offset >= source).astype(jnp.int32)
    counts = counts.at[source, target].set(XW)
    labels = jnp.arange(N_REGION, dtype=jnp.int32)
    counts = jnp.where(labels[:, None] == labels[None, :], 0, counts)
    return counts.astype(jnp.int32)


def set_ends(array, own_key, low, high):
    place = [jax.random.randint(jax.random.fold_in(own_key, axis), (), 0, length) for axis, length in enumerate(array.shape)]
    longest = array.shape.index(max(array.shape))
    next_to = place[:longest] + [(place[longest] + 1) % array.shape[longest]] + place[longest + 1:]
    return array.at[tuple(place)].set(low).at[tuple(next_to)].set(high)


def block_levels(stream_key, shape, shards, least, largest):
    loudness, own = 1.0, jax.random.fold_in(stream_key, 6)
    for dim, shards_of in shards:
        draws = jnp.exp(jax.random.uniform(jax.random.fold_in(own, dim), (shards_of,), jnp.float32, least / len(shards), largest / len(shards)))
        loudness = loudness * jnp.repeat(draws, shape[dim] // shards_of).reshape([-1 if axis == dim else 1 for axis in range(len(shape))])
    return loudness


def setup_inputs(seed: int = 0) -> dict:
    streams_of = jax.random.split(jax.random.key(seed), 15)
    availability = jnp.clip(0.1 + 0.9 * jax.random.uniform(streams_of[0], (HOURS, K, NODES), jnp.float32) ** block_levels(streams_of[0], (HOURS, K, NODES), ((0, 64), (2, 8)), -0.2, 0.2), 0.1, 1.0)
    demand = draw_demand(jax.random.fold_in(streams_of[14], 71), 0)
    gen_cost = jnp.clip(jnp.exp(math.log(1.0) - 2.9957323 * jax.random.uniform(streams_of[2], (K, NODES), jnp.float32) ** block_levels(streams_of[2], (K, NODES), ((1, 8),), -0.2, 0.2)), 0.05, 1.0)
    cap_cost = jnp.clip(jnp.exp(math.log(2048.0) - 2.3025851 * jax.random.uniform(streams_of[3], (N_REGION, COLS), jnp.float32) ** block_levels(streams_of[3], (N_REGION, COLS), ((0, 8), (1, 64)), -0.2, 0.2)), 204.8, 2048.0)
    owner_map = jax.vmap(lambda own: jax.random.permutation(own, COLS))(jax.random.split(streams_of[4], N_REGION)).reshape((N_REGION, COLS)).astype(jnp.int32)
    line_ends = set_ends(jax.random.randint(streams_of[5], (2, LINES), 0, NODE_DEV), jax.random.fold_in(streams_of[5], 1), 0, NODE_DEV - 1).astype(jnp.int32)
    line_limit = jnp.clip(jnp.exp(math.log(4.0) - 2.0794415 * jax.random.uniform(streams_of[6], (LINES,), jnp.float32) ** block_levels(streams_of[6], (LINES,), ((0, 8),), -0.2, 0.2)), 0.5, 4.0)
    cross_ends = set_ends(jax.random.randint(streams_of[7], (2, N_REGION, SLOTS), 0, NODE_DEV), jax.random.fold_in(streams_of[7], 1), 0, NODE_DEV - 1).astype(jnp.int32)
    cross_limit = jnp.clip(jnp.exp(math.log(4.0) - 2.0794415 * jax.random.uniform(streams_of[8], (N_REGION, SLOTS), jnp.float32) ** block_levels(streams_of[8], (N_REGION, SLOTS), ((0, 8),), -0.2, 0.2)), 0.5, 4.0)
    pair_counts = draw_pair_counts(jax.random.fold_in(streams_of[14], 71), 0)
    store_node = set_ends(jax.random.randint(streams_of[10], (STORES,), 0, NODE_DEV), jax.random.fold_in(streams_of[10], 1), 0, NODE_DEV - 1).astype(jnp.int32)
    store_energy = jnp.clip(jnp.exp(math.log(0.4) - 2.9957323 * jax.random.uniform(streams_of[11], (STORES,), jnp.float32) ** block_levels(streams_of[11], (STORES,), ((0, 8),), -0.2, 0.2)), 0.02, 0.4)
    store_power = jnp.clip(jnp.exp(math.log(2.0) - 2.3025851 * jax.random.uniform(streams_of[12], (STORES,), jnp.float32) ** block_levels(streams_of[12], (STORES,), ((0, 8),), -0.2, 0.2)), 0.2, 2.0)
    price_start = jnp.clip(-3.0 + 3.5 * jax.random.uniform(streams_of[13], (HOURS, NODES), jnp.float32) ** block_levels(streams_of[13], (HOURS, NODES), ((0, 64), (1, 8)), -0.2, 0.2), -3.0, 0.5)
    return dict(availability=availability, demand=demand, gen_cost=gen_cost, cap_cost=cap_cost, owner_map=owner_map, line_ends=line_ends, line_limit=line_limit, cross_ends=cross_ends, cross_limit=cross_limit, pair_counts=pair_counts, store_node=store_node, store_energy=store_energy, store_power=store_power, price_start=price_start)


epsilon = 1e-06

def reference(availability, demand, gen_cost, cap_cost, owner_map, line_ends, line_limit, cross_ends, cross_limit, pair_counts, store_node, store_energy, store_power, price_start):
    region_base = jnp.arange(N_REGION, dtype=jnp.int32) * NODE_DEV
    line_region = jnp.arange(LINES, dtype=jnp.int32) // LIN_DEV
    line_from = region_base[line_region] + line_ends[0]
    line_to = region_base[line_region] + line_ends[1]
    slot_ids = jnp.arange(SLOTS, dtype=jnp.int32)
    slot_dest = slot_ids // XW
    cross_from = (region_base[:, None] + cross_ends[0]).reshape(-1)
    cross_to = (region_base[slot_dest][None, :] + cross_ends[1]).reshape(-1)
    slot_used = (slot_ids % XW)[None, :] < pair_counts[:, slot_dest]
    cross_bound = jnp.where(slot_used, cross_limit, 0.0).reshape(-1)
    store_at = region_base[jnp.arange(STORES, dtype=jnp.int32) // S_DEV] + store_node
    region_rows = jnp.arange(N_REGION, dtype=jnp.int32)[:, None]

    def to_dense(owned_values):
        flat_cols = jnp.zeros((N_REGION, COLS), owned_values.dtype).at[region_rows, owner_map].set(owned_values)
        return flat_cols.reshape(N_REGION, K, NODE_DEV).transpose(1, 0, 2).reshape(K, NODES)

    def to_owner(dense_values):
        region_cols = dense_values.reshape(K, N_REGION, NODE_DEV).transpose(1, 0, 2).reshape(N_REGION, COLS)
        return jnp.take_along_axis(region_cols, owner_map, axis=1)
    col_weight = to_owner(lax.optimization_barrier(jnp.sum(availability, axis=0)))
    dispatch = jnp.zeros((HOURS, K, NODES), jnp.float32)
    capacity = jnp.zeros((N_REGION, COLS), jnp.float32)
    inner_flow = jnp.zeros((HOURS, LINES), jnp.float32)
    cross_flow = jnp.zeros((HOURS, N_REGION * SLOTS), jnp.float32)
    discharge = jnp.zeros((HOURS, STORES), jnp.float32)
    charge = jnp.zeros((HOURS, STORES), jnp.float32)
    prices = price_start
    cap_duals = jnp.zeros((HOURS, K, NODES), jnp.float32)
    store_duals = jnp.zeros((HOURS, STORES), jnp.float32)
    weight = jnp.float32(1.0)
    for iteration in range(ITERS):
        primal_step = 0.5 / weight
        dispatch_new = jnp.maximum(dispatch - primal_step * (gen_cost[None] + prices[:, None, :] + cap_duals), 0.0)
        cap_pull = to_owner(lax.optimization_barrier(jnp.sum(availability * cap_duals, axis=0)))
        capacity_new = jnp.maximum(capacity - (cap_cost - cap_pull) / (weight * col_weight), 0.0)
        inner_new = jnp.clip(inner_flow - primal_step * (prices[:, line_to] - prices[:, line_from]), -line_limit, line_limit)
        cross_new = jnp.clip(cross_flow - primal_step * (prices[:, cross_to] - prices[:, cross_from]), -cross_bound, cross_bound)
        discharge_new = jnp.clip(discharge - primal_step * (prices[:, store_at] + store_duals), -store_power, store_power)
        charge_new = jnp.clip(charge - primal_step * (store_duals - jnp.roll(store_duals, -1, axis=0)), 0.0, store_energy)
        dispatch_bar = 2.0 * dispatch_new - dispatch
        capacity_bar = 2.0 * capacity_new - capacity
        inner_bar = 2.0 * inner_new - inner_flow
        cross_bar = 2.0 * cross_new - cross_flow
        discharge_bar = 2.0 * discharge_new - discharge
        charge_bar = 2.0 * charge_new - charge
        balance = lax.optimization_barrier(jnp.sum(dispatch_bar, axis=1))
        balance = balance.at[:, line_to].add(inner_bar).at[:, line_from].add(-inner_bar)
        balance = balance.at[:, cross_to].add(cross_bar).at[:, cross_from].add(-cross_bar)
        balance = balance.at[:, store_at].add(discharge_bar)
        balance = balance - demand
        cap_rows = dispatch_bar - availability * to_dense(capacity_bar)[None]
        storage_rows = charge_bar - jnp.roll(charge_bar, 1, axis=0) + discharge_bar
        prices_new = prices + weight / (K + 8.0) * balance
        cap_new = jnp.maximum(cap_duals + weight / 2.0 * cap_rows, 0.0)
        store_new = store_duals + weight / 3.0 * storage_rows
        if iteration < ITERS - 1:
            primal_sq = jnp.sum((dispatch_new - dispatch) ** 2) + jnp.sum((capacity_new - capacity) ** 2) + jnp.sum((inner_new - inner_flow) ** 2) + jnp.sum((cross_new - cross_flow) ** 2) + jnp.sum((discharge_new - discharge) ** 2) + jnp.sum((charge_new - charge) ** 2)
            dual_sq = jnp.sum((prices_new - prices) ** 2) + jnp.sum((cap_new - cap_duals) ** 2) + jnp.sum((store_new - store_duals) ** 2)
            weight = jnp.sqrt(weight * jnp.sqrt((dual_sq + epsilon) / (primal_sq + epsilon)))
        dispatch, capacity, inner_flow, cross_flow = (dispatch_new, capacity_new, inner_new, cross_new)
        discharge, charge = (discharge_new, charge_new)
        prices, cap_duals, store_duals = (prices_new, cap_new, store_new)
    return (dispatch, capacity, prices, charge)
```

```python
import functools

import jax
import jax.numpy as jnp
from jax import lax
from jax.experimental import pallas as pl
from jax.experimental.pallas import tpu as pltpu
from jax.sharding import PartitionSpec as P

ITERS = 4
PHASES = ITERS - 1
EPSILON = 1e-06
LANES = 128
WIDTH = 32
PARTS = 3
F32 = jnp.float32
BF16 = jnp.bfloat16
MESH = pl.DeviceIdType.MESH


def split(value, parts=PARTS):
    pieces = []
    for part in range(parts):
        piece = value.astype(BF16)
        pieces.append(piece)
        if part + 1 < parts:
            value = value - piece.astype(F32)
    return jnp.concatenate(pieces, axis=0)


def joined(value, parts=PARTS):
    rows = value.shape[0] // parts
    total = value[(parts - 1) * rows :]
    for part in range(parts - 2, -1, -1):
        total = total + value[part * rows : (part + 1) * rows]
    return total


def times(value, matrix):
    product = jnp.dot(split(value), matrix, preferred_element_type=F32)
    return joined(product)


def times_transposed(value, matrix):
    product = lax.dot_general(
        split(value), matrix, (((1,), (1,)), ((), ())), preferred_element_type=F32
    )
    return joined(product)


def fold(value):
    rows, cols = value.shape
    total = value[:, :LANES]
    for tile in range(1, cols // LANES):
        total = total + value[:, tile * LANES : (tile + 1) * LANES]
    if rows > 8:
        total = jnp.sum(total.reshape(rows // 8, 8, LANES), axis=0)
    return jnp.sum(total, axis=0, keepdims=True)


def wait_for(ref, sem):
    pltpu.make_async_copy(ref, ref, sem).wait()


def kernel(
    groups,
    avail,
    demand,
    gen,
    cost,
    owner,
    line_ends,
    line_limit,
    cross_ends,
    cross_limit,
    counts,
    store_node,
    energy,
    power,
    price_start,
    disp,
    cap_out,
    prices,
    charge,
    capd,
    inner,
    discharge,
    sdual,
    cross,
    bal,
    wide,
    local,
    ends_row,
    bound_row,
    msg,
    far,
    info_out,
    info_in,
    start_a,
    start_b,
    col_a,
    col_b,
    sq_a,
    sq_b,
    sq_c,
    halo_out,
    halo_in,
    pad_row,
    msg_send,
    msg_recv,
    info_send,
    info_recv,
    start_send,
    start_recv,
    col_send,
    col_recv,
    sq_send,
    sq_recv,
    halo_send,
    halo_recv,
):
    size_a, size_b, size_r = groups
    hours = size_a * size_b
    rows, tech, nodes = avail.shape
    half = rows // 2
    h = lax.axis_index("hours")
    r = lax.axis_index("region")
    in_a = lax.rem(h, size_a)
    in_b = lax.div(h, size_a)

    def device(hour, region):
        return {"hours": hour, "region": region}

    peers_a = [
        device(in_b * size_a + lax.rem(in_a + j, size_a), r) for j in range(1, size_a)
    ]
    peers_b = [
        device(lax.rem(in_b + j, size_b) * size_a + in_a, r) for j in range(1, size_b)
    ]
    peers_r = [device(h, lax.rem(r + j, size_r)) for j in range(1, size_r)]
    following = device(lax.rem(h + 1, hours), r)
    preceding = device(lax.rem(h + hours - 1, hours), r)

    barrier = pltpu.get_barrier_semaphore()
    everyone = peers_a + peers_b + peers_r + [following, preceding]
    for peer in everyone:
        pl.semaphore_signal(barrier, inc=1, device_id=peer, device_id_type=MESH)
    pl.semaphore_wait(barrier, len(everyone))

    def spread(slots, own, peers, send_sem, recv_sem):
        for peer in peers:
            pltpu.make_async_remote_copy(
                src_ref=slots.at[own],
                dst_ref=slots.at[own],
                send_sem=send_sem,
                recv_sem=recv_sem,
                device_id=peer,
                device_id_type=MESH,
            ).start()

    def collect(slots, peers, sem):
        wait_for(slots.at[pl.ds(0, len(peers))], sem)

    def total(slots):
        value = slots[0]
        for slot in range(1, slots.shape[0]):
            value = value + slots[slot]
        return value

    lane = lax.broadcasted_iota(jnp.int32, (1, LANES), 1)
    leaves = lax.rem(lane, 2 * WIDTH) < WIDTH

    for dest in range(size_r):
        tile = (dest * WIDTH) // LANES * LANES
        place = (dest * WIDTH) % LANES

        def placed(row, first):
            low = pltpu.roll(row, (first - place) % LANES, 1)
            high = pltpu.roll(row, (first + 2 * WIDTH - place) % LANES, 1)
            return jnp.where(lane < 2 * WIDTH, low, high)

        begins = cross_ends[0:1, tile : tile + LANES].astype(F32)
        finish = cross_ends[1:2, tile : tile + LANES].astype(F32)
        used = lax.rem(lane, WIDTH) < counts[0:1, dest : dest + 1]
        bound = jnp.where(used, cross_limit[0:1, tile : tile + LANES], 0.0)
        block = slice(dest * LANES, (dest + 1) * LANES)
        ends_row[:, block] = placed(begins, 0)
        bound_row[:, block] = placed(bound, 0)
        info_out[dest, 0:1] = placed(finish, WIDTH)
        info_out[dest, 1:2] = placed(bound, WIDTH)
    info_in[r] = jnp.zeros(info_in.shape[1:], F32)
    for j in range(1, size_r):
        dest = lax.rem(r + j, size_r)
        pltpu.make_async_remote_copy(
            src_ref=info_out.at[dest],
            dst_ref=info_in.at[r],
            send_sem=info_send,
            recv_sem=info_recv,
            device_id=device(h, dest),
            device_id_type=MESH,
        ).start()

    pad_row[...] = jnp.zeros((1, LANES), F32)
    owned = cost.shape[1]
    pad_row[:, 0:owned] = cost[...]
    per_tile = LANES // owned
    tile = pl.multiple_of(lax.div(h, per_tile) * LANES, LANES)
    cols = owner[0:1, pl.ds(tile, LANES)]
    where_in = lax.rem(h, per_tile)
    mine = cols
    for place in range(1, per_tile):
        moved = pltpu.roll(cols, (LANES - place * owned) % LANES, 1)
        mine = jnp.where(where_in == place, moved, mine)
    mine = jnp.where(lane < owned, mine, -1)
    col_tech = jnp.where(mine < 0, -1, lax.shift_right_arithmetic(mine, 7))
    col_node = jnp.where(mine < 0, -1, lax.rem(mine, nodes))
    node_iota = lax.broadcasted_iota(jnp.int32, (nodes, LANES), 0)
    tech_iota = lax.broadcasted_iota(jnp.int32, (tech, LANES), 0)
    col_hot = jnp.where(col_node == node_iota, 1.0, 0.0).astype(BF16)
    tech_hot = jnp.where(col_tech == tech_iota, 1.0, 0.0)
    start_a[in_a, tech:] = times_transposed(tech_hot * pad_row[...], col_hot)

    def add_hours(i, value):
        part = avail[pl.ds(i * 8, 8)]
        return value + jnp.sum(part, axis=0)

    start_a[in_a, :tech] = lax.fori_loop(
        0, rows // 8, add_hours, jnp.zeros((tech, nodes), F32)
    )
    spread(start_a, in_a, peers_a, start_send.at[0], start_recv.at[0])

    lines = line_limit.shape[1]
    units = energy.shape[1]
    line_iota = lax.broadcasted_iota(jnp.int32, (nodes, lines), 0)
    local[:, :lines] = (
        jnp.where(line_ends[1:2] == line_iota, 1.0, 0.0)
        - jnp.where(line_ends[0:1] == line_iota, 1.0, 0.0)
    ).astype(BF16)
    local[:, lines:] = jnp.where(store_node[...] == line_iota, 1.0, 0.0).astype(BF16)
    disp[...] = jnp.zeros(disp.shape, F32)
    capd[...] = jnp.zeros(capd.shape, F32)
    inner[...] = jnp.zeros(inner.shape, F32)
    discharge[...] = jnp.zeros(discharge.shape, F32)
    charge[...] = jnp.zeros(charge.shape, F32)
    sdual[...] = jnp.zeros(sdual.shape, F32)
    cross[...] = jnp.zeros(cross.shape, F32)
    prices[...] = price_start[...]

    collect(info_in, peers_r, info_recv)
    for dest in range(size_r):
        block = slice(dest * LANES, (dest + 1) * LANES)
        node_row = jnp.where(leaves, ends_row[:, block], info_in[dest, 0:1]).astype(jnp.int32)
        bound_row[:, block] = jnp.where(leaves, bound_row[:, block], info_in[dest, 1:2])
        hot = jnp.where(
            node_row == node_iota, jnp.where(leaves, -1.0, 1.0), 0.0
        )
        wide[:nodes, block] = jnp.where(lane < 2 * WIDTH, hot, 0.0).astype(BF16)
        wide[nodes:, block] = jnp.where(lane < 2 * WIDTH, 0.0, hot).astype(BF16)

    def send_duals(phase, values):
        packed = jnp.concatenate([values[:half], values[half:]], axis=1)
        near = times(packed, wide[...])
        for dest in range(size_r):
            msg[phase, dest] = near[:, dest * LANES : (dest + 1) * LANES]
        far[phase, r] = jnp.zeros((half, LANES), F32)
        for j in range(1, size_r):
            dest = lax.rem(r + j, size_r)
            pltpu.make_async_remote_copy(
                src_ref=msg.at[phase, dest],
                dst_ref=far.at[phase, r],
                send_sem=msg_send.at[phase],
                recv_sem=msg_recv.at[phase],
                device_id=device(h, dest),
                device_id_type=MESH,
            ).start()

    def slot_gaps(phase):
        collect(far.at[phase], peers_r, msg_recv.at[phase])
        gaps = []
        for dest in range(size_r):
            block = far[phase, dest]
            swapped = jnp.where(
                leaves, pltpu.roll(block, LANES - WIDTH, 1), pltpu.roll(block, WIDTH, 1)
            )
            gaps.append(swapped + msg[phase, dest])
        return jnp.concatenate(gaps, axis=1)

    send_duals(0, price_start[...])
    local_gaps = times(price_start[...], local[...])

    collect(start_a, peers_a, start_recv.at[0])
    start_b[in_b] = total(start_a)
    spread(start_b, in_b, peers_b, start_send.at[1], start_recv.at[1])
    gaps = slot_gaps(0)
    collect(start_b, peers_b, start_recv.at[1])
    both = total(start_b)
    col_weight, col_cost = both[:tech], both[tech:]

    capacity = jnp.zeros((tech, nodes), F32)
    pull = jnp.zeros((tech, nodes), F32)
    last_charge = jnp.zeros((1, units), F32)
    next_dual = jnp.zeros((1, units), F32)
    prev_dual = jnp.zeros((1, units), F32)
    weight = jnp.ones((1, 1), F32)
    unit_rows = lax.broadcasted_iota(jnp.int32, (rows, units), 0)

    for iteration in range(ITERS):
        final = iteration == ITERS - 1
        step = 0.5 / weight
        gap_line, gap_unit = local_gaps[:, :lines], local_gaps[:, lines:]
        bounds = bound_row[...]
        limit = line_limit[...]
        cross_old = cross[...]
        inner_old = inner[...]
        dis_old = discharge[...]
        charge_old = charge[...]
        sd_old = sdual[...]
        cross_new = jnp.clip(cross_old - step * gaps, -bounds, bounds)
        inner_new = jnp.clip(inner_old - step * gap_line, -limit, limit)
        dis_new = jnp.clip(dis_old - step * (gap_unit + sd_old), -power[...], power[...])
        sd_next = jnp.where(
            unit_rows == rows - 1, next_dual, pltpu.roll(sd_old, rows - 1, 0)
        )
        charge_new = jnp.clip(charge_old - step * (sd_old - sd_next), 0.0, energy[...])
        cross_gain = cross_new - cross_old
        inner_gain = inner_new - inner_old
        dis_gain = dis_new - dis_old
        dis_bar = dis_new + dis_gain
        charge[...] = charge_new
        net = times_transposed(cross_new + cross_gain, wide[...])
        flow = jnp.concatenate([inner_new + inner_gain, dis_bar], axis=1)
        bal[...] = (
            jnp.concatenate([net[:, :nodes], net[:, nodes:]], axis=0)
            + times_transposed(flow, local[...])
            - demand[...]
        )
        step_b = jnp.broadcast_to(step, (tech, nodes))
        gen_cost = gen[...]
        cap_new = jnp.maximum(capacity - (col_cost - pull) / (weight * col_weight), 0.0)
        cap_gain = cap_new - capacity
        capacity = cap_new

        if final:

            def last_hours(i, carry):
                here = pl.ds(i * 8, 8)
                old = disp[here]
                new = jnp.maximum(
                    old - step_b * (gen_cost + prices[here][:, None, :] + capd[here]), 0.0
                )
                bal[here] += jnp.sum(new + (new - old), axis=1)
                disp[here] = new
                return carry

            lax.fori_loop(0, rows // 8, last_hours, 0)
            prices[...] = prices[...] + weight / (tech + 8.0) * bal[...]
            break

        cap_bar = cap_new + cap_gain
        half_weight = jnp.broadcast_to(weight / 2.0, (tech, nodes))

        def some_hours(i, carry):
            pull_sum, primal, dual = carry
            here = pl.ds(i * 8, 8)
            share = avail[here]
            old = disp[here]
            dual_old = capd[here]
            new = jnp.maximum(
                old - step_b * (gen_cost + prices[here][:, None, :] + dual_old), 0.0
            )
            gain = new - old
            bar = new + gain
            bal[here] += jnp.sum(bar, axis=1)
            dual_new = jnp.maximum(dual_old + half_weight * (bar - share * cap_bar), 0.0)
            dual_gain = dual_new - dual_old
            disp[here] = new
            capd[here] = dual_new
            return (
                pull_sum + jnp.sum(share * dual_new, axis=0),
                primal + jnp.sum(gain * gain, axis=0),
                dual + jnp.sum(dual_gain * dual_gain, axis=0),
            )

        zero = jnp.zeros((tech, nodes), F32)
        pull_sum, primal, dual = lax.fori_loop(0, rows // 8, some_hours, (zero, zero, zero))

        cross[...] = cross_new
        inner[...] = inner_new
        discharge[...] = dis_new
        charge_gain = charge_new - charge_old
        charge_bar = charge_new + charge_gain
        last_new = jnp.clip(last_charge - step * (prev_dual - sd_old[0:1]), 0.0, energy[...])
        last_bar = last_new + (last_new - last_charge)
        last_charge = last_new
        before = jnp.where(unit_rows == 0, last_bar, pltpu.roll(charge_bar, 1, 0))
        sd_gain = weight / 3.0 * (charge_bar - before + dis_bar)
        sd_new = sd_old + sd_gain
        sdual[...] = sd_new
        price_old = prices[...]
        price_new = price_old + weight / (tech + 8.0) * bal[...]
        prices[...] = price_new
        price_gain = price_new - price_old

        leaving = jnp.where(leaves, 1.0, 0.0)
        cross_sq = fold(cross_gain * cross_gain) * leaving
        primal_row = (
            fold(primal)
            + fold(cap_gain * cap_gain) * (1.0 / hours)
            + fold(inner_gain * inner_gain)
            + cross_sq
            + fold(dis_gain * dis_gain)
            + fold(charge_gain * charge_gain)
        )
        sd_step = sd_new - sd_old
        dual_row = fold(dual) + fold(price_gain * price_gain) + fold(sd_step * sd_step)
        sq_a[iteration, in_b, 0:1] = primal_row
        sq_a[iteration, in_b, 1:2] = dual_row
        spread(
            sq_a.at[iteration], in_b, peers_b, sq_send.at[iteration, 0], sq_recv.at[iteration, 0]
        )
        col_a[iteration, in_a] = pull_sum
        spread(
            col_a.at[iteration],
            in_a,
            peers_a,
            col_send.at[iteration, 0],
            col_recv.at[iteration, 0],
        )
        halo_out[iteration, 0] = sd_new[0:1]
        halo_out[iteration, 1] = sd_new[rows - 1 : rows]
        for side, peer in ((0, preceding), (1, following)):
            pltpu.make_async_remote_copy(
                src_ref=halo_out.at[iteration, side],
                dst_ref=halo_in.at[iteration, side],
                send_sem=halo_send.at[iteration, side],
                recv_sem=halo_recv.at[iteration, side],
                device_id=peer,
                device_id_type=MESH,
            ).start()
        send_duals(iteration + 1, price_new)

        collect(sq_a.at[iteration], peers_b, sq_recv.at[iteration, 0])
        sq_b[iteration, in_a] = total(sq_a.at[iteration])
        spread(
            sq_b.at[iteration], in_a, peers_a, sq_send.at[iteration, 1], sq_recv.at[iteration, 1]
        )
        collect(col_a.at[iteration], peers_a, col_recv.at[iteration, 0])
        col_b[iteration, in_b] = total(col_a.at[iteration])
        spread(
            col_b.at[iteration],
            in_b,
            peers_b,
            col_send.at[iteration, 1],
            col_recv.at[iteration, 1],
        )
        local_gaps = times(price_new, local[...])
        collect(sq_b.at[iteration], peers_a, sq_recv.at[iteration, 1])
        sq_c[iteration, r] = total(sq_b.at[iteration])
        spread(
            sq_c.at[iteration], r, peers_r, sq_send.at[iteration, 2], sq_recv.at[iteration, 2]
        )
        collect(col_b.at[iteration], peers_b, col_recv.at[iteration, 1])
        pull = total(col_b.at[iteration])
        gaps = slot_gaps(iteration + 1)
        wait_for(halo_in.at[iteration, 0], halo_recv.at[iteration, 0])
        wait_for(halo_in.at[iteration, 1], halo_recv.at[iteration, 1])
        next_dual = halo_in[iteration, 0]
        prev_dual = halo_in[iteration, 1]
        collect(sq_c.at[iteration], peers_r, sq_recv.at[iteration, 2])
        sums = jnp.sum(total(sq_c.at[iteration]), axis=1, keepdims=True)
        ratio = (sums[1:2] + EPSILON) / (sums[0:1] + EPSILON)
        weight = jnp.sqrt(weight * jnp.sqrt(ratio))

    picked = times(capacity, col_hot) * tech_hot
    cap_out[...] = jnp.sum(picked, axis=0, keepdims=True)[:, :owned]

    collect(info_in, peers_r, info_send)
    collect(start_a, peers_a, start_send.at[0])
    collect(start_b, peers_b, start_send.at[1])
    for phase in range(ITERS):
        collect(far.at[phase], peers_r, msg_send.at[phase])
    for phase in range(PHASES):
        collect(sq_a.at[phase], peers_b, sq_send.at[phase, 0])
        collect(sq_b.at[phase], peers_a, sq_send.at[phase, 1])
        collect(sq_c.at[phase], peers_r, sq_send.at[phase, 2])
        collect(col_a.at[phase], peers_a, col_send.at[phase, 0])
        collect(col_b.at[phase], peers_b, col_send.at[phase, 1])
        for side in range(2):
            wait_for(halo_out.at[phase, side], halo_send.at[phase, side])


def body(
    availability,
    demand,
    gen_cost,
    cap_cost,
    owner_map,
    line_ends,
    line_limit,
    cross_ends,
    cross_limit,
    pair_counts,
    store_node,
    store_energy,
    store_power,
    price_start,
):
    rows, tech, nodes = availability.shape
    lines = line_limit.shape[0]
    units = store_node.shape[0]
    regions = lax.axis_size("region")
    hours = lax.axis_size("hours")
    size_a = 8 if hours % 64 == 0 else 2
    size_b = hours // size_a
    half = rows // 2
    slots = regions * LANES
    dma = pltpu.SemaphoreType.DMA
    scratch = [
        pltpu.VMEM((rows, tech, nodes), F32),
        pltpu.VMEM((rows, lines), F32),
        pltpu.VMEM((rows, units), F32),
        pltpu.VMEM((rows, units), F32),
        pltpu.VMEM((half, slots), F32),
        pltpu.VMEM((rows, nodes), F32),
        pltpu.VMEM((2 * nodes, slots), BF16),
        pltpu.VMEM((nodes, lines + units), BF16),
        pltpu.VMEM((1, slots), F32),
        pltpu.VMEM((1, slots), F32),
        pltpu.VMEM((ITERS, regions, half, LANES), F32),
        pltpu.VMEM((ITERS, regions, half, LANES), F32),
        pltpu.VMEM((regions, 2, LANES), F32),
        pltpu.VMEM((regions, 2, LANES), F32),
        pltpu.VMEM((size_a, 2 * tech, nodes), F32),
        pltpu.VMEM((size_b, 2 * tech, nodes), F32),
        pltpu.VMEM((PHASES, size_a, tech, nodes), F32),
        pltpu.VMEM((PHASES, size_b, tech, nodes), F32),
        pltpu.VMEM((PHASES, size_b, 2, LANES), F32),
        pltpu.VMEM((PHASES, size_a, 2, LANES), F32),
        pltpu.VMEM((PHASES, regions, 2, LANES), F32),
        pltpu.VMEM((PHASES, 2, 1, units), F32),
        pltpu.VMEM((PHASES, 2, 1, units), F32),
        pltpu.VMEM((1, LANES), F32),
        dma((ITERS,)),
        dma((ITERS,)),
        dma(()),
        dma(()),
        dma((2,)),
        dma((2,)),
        dma((PHASES, 2)),
        dma((PHASES, 2)),
        dma((PHASES, 3)),
        dma((PHASES, 3)),
        dma((PHASES, 2)),
        dma((PHASES, 2)),
    ]
    vmem = pl.BlockSpec(memory_space=pltpu.VMEM)
    outs = pl.pallas_call(
        functools.partial(kernel, (size_a, size_b, regions)),
        out_shape=(
            jax.ShapeDtypeStruct((rows, tech, nodes), F32),
            jax.ShapeDtypeStruct(cap_cost.shape, F32),
            jax.ShapeDtypeStruct((rows, nodes), F32),
            jax.ShapeDtypeStruct((rows, units), F32),
        ),
        in_specs=[vmem] * 14,
        out_specs=(vmem,) * 4,
        scratch_shapes=scratch,
        compiler_params=pltpu.CompilerParams(
            collective_id=0, has_side_effects=True, vmem_limit_bytes=40 * 1024 * 1024
        ),
    )(
        availability,
        demand,
        gen_cost,
        cap_cost,
        owner_map,
        line_ends,
        line_limit[None],
        cross_ends[:, 0],
        cross_limit,
        pair_counts,
        store_node[None],
        store_energy[None],
        store_power[None],
        price_start,
    )
    return outs


def solution(mesh):
    placed = (
        P("hours", None, "region"),
        P("hours", "region"),
        P(None, "region"),
        P("region", "hours"),
        P("region", None),
        P(None, "region"),
        P("region"),
        P(None, "region", None),
        P("region", None),
        P("region", None),
        P("region"),
        P("region"),
        P("region"),
        P("hours", "region"),
    )
    return jax.shard_map(
        body,
        mesh=mesh,
        in_specs=placed,
        out_specs=(
            P("hours", None, "region"),
            P("region", "hours"),
            P("hours", "region"),
            P("hours", "region"),
        ),
        check_vma=False,
    )
```

```python
import functools

import jax
import jax.numpy as jnp
from jax import lax
from jax.experimental import pallas as pl
from jax.experimental.pallas import tpu as pltpu
from jax.sharding import PartitionSpec as P

ITERS = 4
PHASES = ITERS - 1
PIECES = 4
EPSILON = 1e-06
LANES = 128
WIDTH = 32
PARTS = 3
F32 = jnp.float32
BF16 = jnp.bfloat16
MESH = pl.DeviceIdType.MESH


def split(value, parts=PARTS):
    pieces = []
    for part in range(parts):
        piece = value.astype(BF16)
        pieces.append(piece)
        if part + 1 < parts:
            value = value - piece.astype(F32)
    return jnp.concatenate(pieces, axis=0)


def joined(value, parts=PARTS):
    rows = value.shape[0] // parts
    total = value[(parts - 1) * rows :]
    for part in range(parts - 2, -1, -1):
        total = total + value[part * rows : (part + 1) * rows]
    return total


def times(value, matrix):
    product = jnp.dot(split(value), matrix, preferred_element_type=F32)
    return joined(product)


def times_transposed(value, matrix):
    product = lax.dot_general(
        split(value), matrix, (((1,), (1,)), ((), ())), preferred_element_type=F32
    )
    return joined(product)


def fold(value):
    rows, cols = value.shape
    total = value[:, :LANES]
    for tile in range(1, cols // LANES):
        total = total + value[:, tile * LANES : (tile + 1) * LANES]
    if rows > 8:
        total = jnp.sum(total.reshape(rows // 8, 8, LANES), axis=0)
    return jnp.sum(total, axis=0, keepdims=True)


def wait_for(ref, sem):
    pltpu.make_async_copy(ref, ref, sem).wait()


def kernel(groups, *refs):
    sources, results, inputs = refs[:14], refs[14:18], refs[18:32]
    steps(groups, sources, results, inputs, *inputs, *refs[32:])


def steps(
    groups,
    sources,
    results,
    inputs,
    avail,
    demand,
    gen,
    cost,
    owner,
    line_ends,
    line_limit,
    cross_ends,
    cross_limit,
    counts,
    store_node,
    energy,
    power,
    price_start,
    in_sem,
    out_sem,
    disp,
    cap_row,
    prices,
    charge,
    capd,
    slope,
    inner,
    discharge,
    sdual,
    cross,
    bal,
    wide,
    wide_far,
    local,
    ends_row,
    far_row,
    bound_row,
    raw,
    msg,
    far,
    info_out,
    info_in,
    start_a,
    start_b,
    col_a,
    col_b,
    sq_a,
    sq_b,
    halo_out,
    halo_in,
    pad_row,
    raw_send,
    raw_recv,
    msg_send,
    msg_recv,
    info_send,
    info_recv,
    start_send,
    start_recv,
    col_send,
    col_recv,
    sq_send,
    sq_recv,
    halo_send,
    halo_recv,
):
    size_x, size_z, size_r = groups
    cores = 2
    size_a, size_b = size_x * cores, size_z
    hours = size_a * size_b
    rows, tech, nodes = avail.shape
    half = rows // 2
    h = lax.axis_index("hours")
    r = lax.axis_index("region")
    core = lax.rem(h, cores)
    in_a = lax.rem(h, size_a)
    in_x = lax.div(in_a, cores)
    in_b = lax.div(h, size_a)

    def device(hour, region):
        return {"hours": hour, "region": region}

    def others(first, second):
        def hops(step):
            return min(step[0], first - step[0]) + min(step[1], second - step[1])

        pairs = [(i, j) for i in range(first) for j in range(second) if i or j]
        return sorted(pairs, key=hops, reverse=True)

    peers_a = [
        device(in_b * size_a + lax.rem(in_a + j, size_a), r) for j in range(1, size_a)
    ]
    peers_b = [
        device(lax.rem(in_b + j, size_b) * size_a + in_a, r) for j in range(1, size_b)
    ]
    peers_r = [device(h, lax.rem(r + j, size_r)) for j in range(1, size_r)]
    peers_zx = [
        device(
            lax.rem(in_b + i, size_z) * size_a + lax.rem(in_x + j, size_x) * cores + core, r
        )
        for i, j in others(size_z, size_x)
    ]
    peers_rc = [
        device(h - core + lax.rem(core + j, cores), lax.rem(r + i, size_r))
        for i, j in others(size_r, cores)
    ]
    following = device(lax.rem(h + 1, hours), r)
    preceding = device(lax.rem(h + hours - 1, hours), r)

    barrier = pltpu.get_barrier_semaphore()
    everyone = peers_zx + peers_rc + peers_a + [following, preceding]
    for peer in everyone:
        pl.semaphore_signal(barrier, inc=1, device_id=peer, device_id_type=MESH)
    arriving = [
        pltpu.make_async_copy(source, target, in_sem.at[place])
        for place, (source, target) in enumerate(zip(sources, inputs))
    ]
    early = (0, 7, 8, 9, 3, 4)
    late = [place for place in range(len(inputs)) if place not in early]
    for place in (*early, *late):
        arriving[place].start()

    def spread(slots, own, peers, send_sem, recv_sem):
        for peer in peers:
            pltpu.make_async_remote_copy(
                src_ref=slots.at[own],
                dst_ref=slots.at[own],
                send_sem=send_sem,
                recv_sem=recv_sem,
                device_id=peer,
                device_id_type=MESH,
            ).start()

    def collect(slots, peers, sem):
        wait_for(slots.at[pl.ds(0, len(peers))], sem)

    def total(slots):
        values = [slots[slot] for slot in range(slots.shape[0])]
        while len(values) > 1:
            values = [
                sum(values[at + 1 : at + 2], values[at]) for at in range(0, len(values), 2)
            ]
        return values[0]

    lane = lax.broadcasted_iota(jnp.int32, (1, LANES), 1)
    leaves = lax.rem(lane, 2 * WIDTH) < WIDTH

    for place in early:
        arriving[place].wait()
    for dest in range(size_r):
        tile = (dest * WIDTH) // LANES * LANES
        place = (dest * WIDTH) % LANES

        def placed(row, first):
            low = pltpu.roll(row, (first - place) % LANES, 1)
            high = pltpu.roll(row, (first + 2 * WIDTH - place) % LANES, 1)
            return jnp.where(lane < 2 * WIDTH, low, high)

        begins = cross_ends[0, :, tile : tile + LANES].astype(F32)
        finish = cross_ends[1, :, tile : tile + LANES].astype(F32)
        used = lax.rem(lane, WIDTH) < counts[0:1, dest : dest + 1]
        bound = jnp.where(used, cross_limit[0:1, tile : tile + LANES], 0.0)
        block = slice(dest * LANES, (dest + 1) * LANES)
        ends_row[:, block] = placed(begins, 0)
        far_row[:, block] = placed(finish, 0)
        bound_row[:, block] = placed(bound, 0)
        info_out[dest, 0:1] = placed(finish, WIDTH)
        info_out[dest, 1:2] = placed(bound, WIDTH)
        info_out[dest, 2:3] = placed(begins, WIDTH)
        info_out[dest, 3:4] = jnp.zeros((1, LANES), F32)
    info_in[r] = jnp.zeros(info_in.shape[1:], F32)
    raw[r] = jnp.zeros(raw.shape[1:], F32)

    pad_row[...] = jnp.zeros((1, LANES), F32)
    owned = cost.shape[1]
    pad_row[:, 0:owned] = cost[...]
    per_tile = LANES // owned
    tile = pl.multiple_of(lax.div(h, per_tile) * LANES, LANES)
    cols = owner[0:1, pl.ds(tile, LANES)]
    where_in = lax.rem(h, per_tile)
    mine = cols
    for place in range(1, per_tile):
        moved = pltpu.roll(cols, (LANES - place * owned) % LANES, 1)
        mine = jnp.where(where_in == place, moved, mine)
    mine = jnp.where(lane < owned, mine, -1)
    col_tech = jnp.where(mine < 0, -1, lax.shift_right_arithmetic(mine, 7))
    col_node = jnp.where(mine < 0, -1, lax.rem(mine, nodes))
    node_iota = lax.broadcasted_iota(jnp.int32, (nodes, LANES), 0)
    tech_iota = lax.broadcasted_iota(jnp.int32, (tech, LANES), 0)
    col_hot = jnp.where(col_node == node_iota, 1.0, 0.0).astype(BF16)
    tech_hot = jnp.where(col_tech == tech_iota, 1.0, 0.0)
    start_a[in_a, tech:] = times_transposed(tech_hot * pad_row[...], col_hot)

    def add_hours(i, value):
        part = avail[pl.ds(i * 8, 8)]
        return value + jnp.sum(part, axis=0)

    start_a[in_a, :tech] = lax.fori_loop(
        0, rows // 8, add_hours, jnp.zeros((tech, nodes), F32)
    )

    pl.semaphore_wait(barrier, len(everyone))
    spread(start_a, in_a, peers_a, start_send.at[0], start_recv.at[0])
    for j in range(1, size_r):
        dest = lax.rem(r + j, size_r)
        pltpu.make_async_remote_copy(
            src_ref=info_out.at[dest],
            dst_ref=info_in.at[r],
            send_sem=info_send,
            recv_sem=info_recv,
            device_id=device(h, dest),
            device_id_type=MESH,
        ).start()
    for peer in peers_r:
        pltpu.make_async_remote_copy(
            src_ref=sources[13],
            dst_ref=raw.at[r],
            send_sem=raw_send,
            recv_sem=raw_recv,
            device_id=peer,
            device_id_type=MESH,
        ).start()
    for place in late:
        arriving[place].wait()

    lines = line_limit.shape[1]
    units = energy.shape[1]
    line_iota = lax.broadcasted_iota(jnp.int32, (nodes, lines), 0)
    local[:, :lines] = (
        jnp.where(line_ends[1:2] == line_iota, 1.0, 0.0)
        - jnp.where(line_ends[0:1] == line_iota, 1.0, 0.0)
    ).astype(BF16)
    local[:, lines:] = jnp.where(store_node[...] == line_iota, 1.0, 0.0).astype(BF16)
    local_gaps = times(price_start[...], local[...])

    def first_dispatch(i, primal):
        here = pl.ds(i * 8, 8)
        new = jnp.maximum(-0.5 * (gen[...] + price_start[here][:, None, :]), 0.0)
        disp[here] = new
        bal[here] = jnp.sum(new + new, axis=1) - demand[here]
        return primal + jnp.sum(new * new, axis=0)

    zero = jnp.zeros((tech, nodes), F32)
    primal = lax.fori_loop(0, rows // 8, first_dispatch, zero)

    collect(start_a, peers_a, start_recv.at[0])
    start_b[in_b] = total(start_a)
    spread(start_b, in_b, peers_b, start_send.at[1], start_recv.at[1])

    collect(info_in, peers_r, info_recv)
    for dest in range(size_r):
        block = slice(dest * LANES, (dest + 1) * LANES)
        near_at = jnp.where(leaves, ends_row[:, block], info_in[dest, 0:1]).astype(jnp.int32)
        far_at = jnp.where(leaves, far_row[:, block], info_in[dest, 2:3]).astype(jnp.int32)
        bound_row[:, block] = jnp.where(leaves, bound_row[:, block], info_in[dest, 1:2])
        sign = jnp.where(leaves, -1.0, 1.0)
        hot = jnp.where(near_at == node_iota, sign, 0.0)
        wide[:nodes, block] = jnp.where(lane < 2 * WIDTH, hot, 0.0).astype(BF16)
        wide[nodes:, block] = jnp.where(lane < 2 * WIDTH, 0.0, hot).astype(BF16)
        hot = jnp.where(far_at == node_iota, -sign, 0.0)
        wide_far[:nodes, block] = jnp.where(lane < 2 * WIDTH, hot, 0.0).astype(BF16)
        wide_far[nodes:, block] = jnp.where(lane < 2 * WIDTH, 0.0, hot).astype(BF16)

    def packed(values):
        return jnp.concatenate([values[:half], values[half:]], axis=1)

    near = times(packed(price_start[...]), wide[...])
    collect(raw, peers_r, raw_recv)
    gaps = near + jnp.concatenate(
        [
            times(packed(raw[dest]), wide_far[:, dest * LANES : (dest + 1) * LANES])
            for dest in range(size_r)
        ],
        axis=1,
    )

    def send_duals(phase, values):
        near = times(packed(values), wide[...])
        for dest in range(size_r):
            msg[phase, dest] = near[:, dest * LANES : (dest + 1) * LANES]
        far[phase, r] = jnp.zeros((half, LANES), F32)
        for j in range(1, size_r):
            dest = lax.rem(r + j, size_r)
            pltpu.make_async_remote_copy(
                src_ref=msg.at[phase, dest],
                dst_ref=far.at[phase, r],
                send_sem=msg_send.at[phase],
                recv_sem=msg_recv.at[phase],
                device_id=device(h, dest),
                device_id_type=MESH,
            ).start()

    def slot_gaps(phase):
        collect(far.at[phase], peers_r, msg_recv.at[phase])
        gaps = []
        for dest in range(size_r):
            block = far[phase, dest]
            swapped = jnp.where(
                leaves, pltpu.roll(block, LANES - WIDTH, 1), pltpu.roll(block, WIDTH, 1)
            )
            gaps.append(swapped + msg[phase, dest])
        return jnp.concatenate(gaps, axis=1)

    capacity = zero
    pull = zero
    last_charge = jnp.zeros((1, units), F32)
    next_dual = jnp.zeros((1, units), F32)
    prev_dual = jnp.zeros((1, units), F32)
    weight = jnp.ones((1, 1), F32)
    unit_rows = lax.broadcasted_iota(jnp.int32, (rows, units), 0)
    cross_old = jnp.zeros(cross.shape, F32)
    inner_old = jnp.zeros(inner.shape, F32)
    dis_old = jnp.zeros(discharge.shape, F32)
    charge_old = jnp.zeros(charge.shape, F32)
    sd_old = jnp.zeros(sdual.shape, F32)
    price_old = price_start[...]

    for iteration in range(ITERS):
        start = iteration == 0
        final = iteration == ITERS - 1
        step = 0.5 / weight
        gap_line, gap_unit = local_gaps[:, :lines], local_gaps[:, lines:]
        bounds = bound_row[...]
        limit = line_limit[...]
        if not start:
            cross_old = cross[...]
            inner_old = inner[...]
            dis_old = discharge[...]
            charge_old = charge[...]
            sd_old = sdual[...]
            price_old = prices[...]
        cross_new = jnp.clip(cross_old - step * gaps, -bounds, bounds)
        inner_new = jnp.clip(inner_old - step * gap_line, -limit, limit)
        dis_new = jnp.clip(dis_old - step * (gap_unit + sd_old), -power[...], power[...])
        sd_next = jnp.where(
            unit_rows == rows - 1, next_dual, pltpu.roll(sd_old, rows - 1, 0)
        )
        charge_new = jnp.clip(charge_old - step * (sd_old - sd_next), 0.0, energy[...])
        cross_gain = cross_new - cross_old
        inner_gain = inner_new - inner_old
        dis_gain = dis_new - dis_old
        dis_bar = dis_new + dis_gain
        charge[...] = charge_new
        net = times_transposed(cross_new + cross_gain, wide[...])
        flow = jnp.concatenate([inner_new + inner_gain, dis_bar], axis=1)
        moved = jnp.concatenate(
            [net[:, :nodes], net[:, nodes:]], axis=0
        ) + times_transposed(flow, local[...])
        step_b = jnp.broadcast_to(step, (tech, nodes))

        def new_capacity():
            return jnp.maximum(capacity - (col_cost - pull) / (weight * col_weight), 0.0)

        if final:
            pltpu.make_async_copy(charge, results[3], out_sem.at[3]).start()
            capacity = new_capacity()
            picked = times(capacity, col_hot) * tech_hot
            cap_row[...] = jnp.sum(picked, axis=0, keepdims=True)[:, :owned]
            pltpu.make_async_copy(cap_row, results[1], out_sem.at[1]).start()

            def last_hours(i, carry):
                here = pl.ds(i * 8, 8)
                old = disp[here]
                new = jnp.maximum(old - step_b * slope[here], 0.0)
                bal[here] = jnp.sum(new + (new - old), axis=1) - demand[here]
                disp[here] = new
                pltpu.make_async_copy(
                    disp.at[here], results[0].at[here], out_sem.at[0]
                ).start()
                return carry

            lax.fori_loop(0, rows // 8, last_hours, 0)
            prices[...] = price_old + weight / (tech + 8.0) * (bal[...] + moved)
            pltpu.make_async_copy(prices, results[2], out_sem.at[2]).start()
            break

        half_weight = jnp.broadcast_to(weight / 2.0, (tech, nodes))
        if start:
            price_new = price_old + weight / (tech + 8.0) * (bal[...] + moved)
            send_duals(1, price_new)
            collect(start_b, peers_b, start_recv.at[1])
            both = total(start_b)
            col_weight, col_cost = both[:tech], both[tech:]
            cap_new = new_capacity()
            cap_gain = cap_new - capacity
            cap_bar = cap_new + cap_gain

            def first_duals(i, dual):
                here = pl.ds(i * 8, 8)
                new = disp[here]
                dual_new = jnp.maximum(
                    half_weight * (new + new - avail[here] * cap_bar), 0.0
                )
                capd[here] = dual_new
                return dual + jnp.sum(dual_new * dual_new, axis=0)

            dual = lax.fori_loop(0, rows // 8, first_duals, zero)
        else:
            cap_new = new_capacity()
            cap_gain = cap_new - capacity
            cap_bar = cap_new + cap_gain

            def some_hours(i, carry):
                primal, dual = carry
                here = pl.ds(i * 8, 8)
                old = disp[here]
                dual_old = capd[here]
                new = jnp.maximum(old - step_b * slope[here], 0.0)
                gain = new - old
                bar = new + gain
                bal[here] = jnp.sum(bar, axis=1) - demand[here]
                dual_new = jnp.maximum(
                    dual_old + half_weight * (bar - avail[here] * cap_bar), 0.0
                )
                dual_gain = dual_new - dual_old
                disp[here] = new
                capd[here] = dual_new
                return (
                    primal + jnp.sum(gain * gain, axis=0),
                    dual + jnp.sum(dual_gain * dual_gain, axis=0),
                )

            primal, dual = lax.fori_loop(0, rows // 8, some_hours, (zero, zero))
            price_new = price_old + weight / (tech + 8.0) * (bal[...] + moved)

        capacity = cap_new
        charge_gain = charge_new - charge_old
        charge_bar = charge_new + charge_gain
        last_new = jnp.clip(last_charge - step * (prev_dual - sd_old[0:1]), 0.0, energy[...])
        last_bar = last_new + (last_new - last_charge)
        last_charge = last_new
        before = jnp.where(unit_rows == 0, last_bar, pltpu.roll(charge_bar, 1, 0))
        sd_gain = weight / 3.0 * (charge_bar - before + dis_bar)
        sd_new = sd_old + sd_gain
        price_gain = price_new - price_old

        leaving = jnp.where(leaves, 1.0, 0.0)
        cross_sq = fold(cross_gain * cross_gain) * leaving
        primal_row = (
            fold(primal)
            + fold(cap_gain * cap_gain) * (1.0 / hours)
            + fold(inner_gain * inner_gain)
            + cross_sq
            + fold(dis_gain * dis_gain)
            + fold(charge_gain * charge_gain)
        )
        sd_step = sd_new - sd_old
        dual_row = fold(dual) + fold(price_gain * price_gain) + fold(sd_step * sd_step)
        in_zx = in_b * size_x + in_x
        sq_a[iteration, in_zx, 0:1] = primal_row
        sq_a[iteration, in_zx, 1:2] = dual_row
        spread(
            sq_a.at[iteration],
            in_zx,
            peers_zx,
            sq_send.at[iteration, 0],
            sq_recv.at[iteration, 0],
        )

        cross[...] = cross_new
        inner[...] = inner_new
        discharge[...] = dis_new
        sdual[...] = sd_new
        prices[...] = price_new

        def prepare(i, pull_sum):
            here = pl.ds(i * 8, 8)
            dual_now = capd[here]
            slope[here] = gen[...] + prices[here][:, None, :] + dual_now
            return pull_sum + jnp.sum(avail[here] * dual_now, axis=0)

        col_a[iteration, in_a] = lax.fori_loop(0, rows // 8, prepare, zero)
        spread(
            col_a.at[iteration],
            in_a,
            peers_a,
            col_send.at[iteration, 0],
            col_recv.at[iteration, 0],
        )
        halo_out[iteration, 0] = sd_new[0:1]
        halo_out[iteration, 1] = sd_new[rows - 1 : rows]
        for side, peer in ((0, preceding), (1, following)):
            pltpu.make_async_remote_copy(
                src_ref=halo_out.at[iteration, side],
                dst_ref=halo_in.at[iteration, side],
                send_sem=halo_send.at[iteration, side],
                recv_sem=halo_recv.at[iteration, side],
                device_id=peer,
                device_id_type=MESH,
            ).start()
        if not start:
            send_duals(iteration + 1, price_new)
        local_gaps = times(price_new, local[...])

        collect(col_a.at[iteration], peers_a, col_recv.at[iteration, 0])
        col_b[iteration, in_b] = total(col_a.at[iteration])
        spread(
            col_b.at[iteration],
            in_b,
            peers_b,
            col_send.at[iteration, 1],
            col_recv.at[iteration, 1],
        )
        collect(sq_a.at[iteration], peers_zx, sq_recv.at[iteration, 0])
        in_rc = r * cores + core
        sq_b[iteration, in_rc] = total(sq_a.at[iteration])
        spread(
            sq_b.at[iteration],
            in_rc,
            peers_rc,
            sq_send.at[iteration, 1],
            sq_recv.at[iteration, 1],
        )
        gaps = slot_gaps(iteration + 1)
        wait_for(halo_in.at[iteration, 0], halo_recv.at[iteration, 0])
        wait_for(halo_in.at[iteration, 1], halo_recv.at[iteration, 1])
        next_dual = halo_in[iteration, 0]
        prev_dual = halo_in[iteration, 1]
        collect(col_b.at[iteration], peers_b, col_recv.at[iteration, 1])
        pull = total(col_b.at[iteration])
        collect(sq_b.at[iteration], peers_rc, sq_recv.at[iteration, 1])
        sums = jnp.sum(total(sq_b.at[iteration]), axis=1, keepdims=True)
        ratio = (sums[1:2] + EPSILON) / (sums[0:1] + EPSILON)
        weight = jnp.sqrt(weight * jnp.sqrt(ratio))

    collect(info_in, peers_r, info_send)
    collect(raw, peers_r, raw_send)
    collect(start_a, peers_a, start_send.at[0])
    collect(start_b, peers_b, start_send.at[1])
    for phase in range(1, ITERS):
        collect(far.at[phase], peers_r, msg_send.at[phase])
    for phase in range(PHASES):
        collect(sq_a.at[phase], peers_zx, sq_send.at[phase, 0])
        collect(sq_b.at[phase], peers_rc, sq_send.at[phase, 1])
        collect(col_a.at[phase], peers_a, col_send.at[phase, 0])
        collect(col_b.at[phase], peers_b, col_send.at[phase, 1])
        for side in range(2):
            wait_for(halo_out.at[phase, side], halo_send.at[phase, side])
    for place, value in enumerate((disp, cap_row, prices, charge)):
        pltpu.make_async_copy(value, results[place], out_sem.at[place]).wait()


def store_outputs(*refs):
    sources, targets, held = refs[:4], refs[4:8], refs[8:12]
    in_sem, out_sem = refs[12:]
    rows = sources[0].shape[0]
    piece = rows // PIECES
    parts = [(0, pl.ds(at * piece, piece)) for at in range(PIECES)]
    parts += [(place, slice(None)) for place in (3, 2, 1)]
    loads, stores = [], []
    for at, (place, here) in enumerate(parts):
        source, target, stage = (
            ref if place else ref.at[here]
            for ref in (sources[place], targets[place], held[place])
        )
        loads.append(pltpu.make_async_copy(source, stage, in_sem.at[at]))
        stores.append(pltpu.make_async_copy(stage, target, out_sem.at[at]))
    for load in loads:
        load.start()
    for load, store in zip(loads, stores):
        load.wait()
        store.start()
    for store in stores:
        store.wait()


def body(
    availability,
    demand,
    gen_cost,
    cap_cost,
    owner_map,
    line_ends,
    line_limit,
    cross_ends,
    cross_limit,
    pair_counts,
    store_node,
    store_energy,
    store_power,
    price_start,
):
    rows, tech, nodes = availability.shape
    lines = line_limit.shape[0]
    units = store_node.shape[0]
    regions = lax.axis_size("region")
    hours = lax.axis_size("hours")
    size_a = 8 if hours % 64 == 0 else 2
    size_b = hours // size_a
    half = rows // 2
    slots = regions * LANES
    dma = pltpu.SemaphoreType.DMA
    arrays = (
        availability,
        demand,
        gen_cost,
        cap_cost,
        owner_map,
        line_ends,
        line_limit[None],
        cross_ends,
        cross_limit,
        pair_counts,
        store_node[None],
        store_energy[None],
        store_power[None],
        price_start,
    )
    scratch = [pltpu.VMEM(array.shape, array.dtype) for array in arrays] + [
        dma((len(arrays),)),
        dma((4,)),
        pltpu.VMEM((rows, tech, nodes), F32),
        pltpu.VMEM(cap_cost.shape, F32),
        pltpu.VMEM((rows, nodes), F32),
        pltpu.VMEM((rows, units), F32),
        pltpu.VMEM((rows, tech, nodes), F32),
        pltpu.VMEM((rows, tech, nodes), F32),
        pltpu.VMEM((rows, lines), F32),
        pltpu.VMEM((rows, units), F32),
        pltpu.VMEM((rows, units), F32),
        pltpu.VMEM((half, slots), F32),
        pltpu.VMEM((rows, nodes), F32),
        pltpu.VMEM((2 * nodes, slots), BF16),
        pltpu.VMEM((2 * nodes, slots), BF16),
        pltpu.VMEM((nodes, lines + units), BF16),
        pltpu.VMEM((1, slots), F32),
        pltpu.VMEM((1, slots), F32),
        pltpu.VMEM((1, slots), F32),
        pltpu.VMEM((regions, rows, nodes), F32),
        pltpu.VMEM((ITERS, regions, half, LANES), F32),
        pltpu.VMEM((ITERS, regions, half, LANES), F32),
        pltpu.VMEM((regions, 4, LANES), F32),
        pltpu.VMEM((regions, 4, LANES), F32),
        pltpu.VMEM((size_a, 2 * tech, nodes), F32),
        pltpu.VMEM((size_b, 2 * tech, nodes), F32),
        pltpu.VMEM((PHASES, size_a, tech, nodes), F32),
        pltpu.VMEM((PHASES, size_b, tech, nodes), F32),
        pltpu.VMEM((PHASES, hours // 2, 2, LANES), F32),
        pltpu.VMEM((PHASES, 2 * regions, 2, LANES), F32),
        pltpu.VMEM((PHASES, 2, 1, units), F32),
        pltpu.VMEM((PHASES, 2, 1, units), F32),
        pltpu.VMEM((1, LANES), F32),
        dma(()),
        dma(()),
        dma((ITERS,)),
        dma((ITERS,)),
        dma(()),
        dma(()),
        dma((2,)),
        dma((2,)),
        dma((PHASES, 2)),
        dma((PHASES, 2)),
        dma((PHASES, 2)),
        dma((PHASES, 2)),
        dma((PHASES, 2)),
        dma((PHASES, 2)),
    ]
    hbm = pl.BlockSpec(memory_space=pltpu.HBM)
    outs = pl.pallas_call(
        functools.partial(kernel, (size_a // 2, size_b, regions)),
        out_shape=(
            jax.ShapeDtypeStruct((rows, tech, nodes), F32),
            jax.ShapeDtypeStruct(cap_cost.shape, F32),
            jax.ShapeDtypeStruct((rows, nodes), F32),
            jax.ShapeDtypeStruct((rows, units), F32),
        ),
        in_specs=[hbm] * len(arrays),
        out_specs=(hbm,) * 4,
        scratch_shapes=scratch,
        compiler_params=pltpu.CompilerParams(
            collective_id=0, has_side_effects=True, vmem_limit_bytes=60 * 1024 * 1024
        ),
    )(*arrays)
    return pl.pallas_call(
        store_outputs,
        out_shape=tuple(jax.ShapeDtypeStruct(out.shape, F32) for out in outs),
        in_specs=[hbm] * 4,
        out_specs=(hbm,) * 4,
        scratch_shapes=[pltpu.VMEM(out.shape, F32) for out in outs]
        + [dma((PIECES + 3,)), dma((PIECES + 3,))],
    )(*outs)


def solution(mesh):
    placed = (
        P("hours", None, "region"),
        P("hours", "region"),
        P(None, "region"),
        P("region", "hours"),
        P("region", None),
        P(None, "region"),
        P("region"),
        P(None, "region", None),
        P("region", None),
        P("region", None),
        P("region"),
        P("region"),
        P("region"),
        P("hours", "region"),
    )
    return jax.shard_map(
        body,
        mesh=mesh,
        in_specs=placed,
        out_specs=(
            P("hours", None, "region"),
            P("region", "hours"),
            P("hours", "region"),
            P("hours", "region"),
        ),
        check_vma=False,
    )
```

```python
import functools

import jax
import jax.numpy as jnp
from jax import lax
from jax.experimental import pallas as pl
from jax.experimental.pallas import tpu as pltpu
from jax.sharding import PartitionSpec as P

ITERS = 4
PHASES = ITERS - 1
EPSILON = 1e-06
LANES = 128
WIDTH = 32
PARTS = 3
F32 = jnp.float32
BF16 = jnp.bfloat16
MESH = pl.DeviceIdType.MESH


def split(value, parts=PARTS):
    pieces = []
    for part in range(parts):
        piece = value.astype(BF16)
        pieces.append(piece)
        if part + 1 < parts:
            value = value - piece.astype(F32)
    return jnp.concatenate(pieces, axis=0)


def joined(value, parts=PARTS):
    rows = value.shape[0] // parts
    total = value[(parts - 1) * rows :]
    for part in range(parts - 2, -1, -1):
        total = total + value[part * rows : (part + 1) * rows]
    return total


def times(value, matrix):
    product = jnp.dot(split(value), matrix, preferred_element_type=F32)
    return joined(product)


def times_transposed(value, matrix):
    product = lax.dot_general(
        split(value), matrix, (((1,), (1,)), ((), ())), preferred_element_type=F32
    )
    return joined(product)


def fold(value):
    rows, cols = value.shape
    total = value[:, :LANES]
    for tile in range(1, cols // LANES):
        total = total + value[:, tile * LANES : (tile + 1) * LANES]
    if rows > 8:
        total = jnp.sum(total.reshape(rows // 8, 8, LANES), axis=0)
    return jnp.sum(total, axis=0, keepdims=True)


def wait_for(ref, sem):
    pltpu.make_async_copy(ref, ref, sem).wait()


def kernel(groups, *refs):
    sources, results, inputs = refs[:14], refs[14:18], refs[18:32]
    steps(groups, sources, inputs, results, *inputs, *refs[32:])


def steps(
    groups,
    sources,
    inputs,
    results,
    avail,
    demand,
    gen,
    cost,
    owner,
    line_ends,
    line_limit,
    cross_ends,
    cross_limit,
    counts,
    store_node,
    energy,
    power,
    price_start,
    in_sem,
    capd,
    slope,
    inner,
    discharge,
    sdual,
    cross,
    bal,
    wide,
    wide_far,
    local,
    ends_row,
    far_row,
    bound_row,
    raw,
    msg,
    far,
    info_out,
    info_in,
    start_a,
    start_b,
    col_a,
    col_b,
    sq_a,
    sq_b,
    halo_out,
    halo_in,
    pad_row,
    raw_send,
    raw_recv,
    msg_send,
    msg_recv,
    info_send,
    info_recv,
    start_send,
    start_recv,
    col_send,
    col_recv,
    sq_send,
    sq_recv,
    halo_send,
    halo_recv,
):
    size_x, size_z, size_r = groups
    disp, cap_row, prices, charge = results
    cores = 2
    size_a, size_b = size_x * cores, size_z
    hours = size_a * size_b
    rows, tech, nodes = avail.shape
    half = rows // 2
    h = lax.axis_index("hours")
    r = lax.axis_index("region")
    core = lax.rem(h, cores)
    in_a = lax.rem(h, size_a)
    in_x = lax.div(in_a, cores)
    in_b = lax.div(h, size_a)

    def device(hour, region):
        return {"hours": hour, "region": region}

    def others(first, second):
        def hops(step):
            return min(step[0], first - step[0]) + min(step[1], second - step[1])

        pairs = [(i, j) for i in range(first) for j in range(second) if i or j]
        return sorted(pairs, key=hops, reverse=True)

    peers_a = [
        device(in_b * size_a + lax.rem(in_a + j, size_a), r) for j in range(1, size_a)
    ]
    peers_b = [
        device(lax.rem(in_b + j, size_b) * size_a + in_a, r) for j in range(1, size_b)
    ]
    peers_r = [device(h, lax.rem(r + j, size_r)) for j in range(1, size_r)]
    peers_zx = [
        device(
            lax.rem(in_b + i, size_z) * size_a + lax.rem(in_x + j, size_x) * cores + core, r
        )
        for i, j in others(size_z, size_x)
    ]
    peers_rc = [
        device(h - core + lax.rem(core + j, cores), lax.rem(r + i, size_r))
        for i, j in others(size_r, cores)
    ]
    following = device(lax.rem(h + 1, hours), r)
    preceding = device(lax.rem(h + hours - 1, hours), r)

    barrier = pltpu.get_barrier_semaphore()
    everyone = peers_b + peers_rc + peers_a
    for peer in everyone:
        pl.semaphore_signal(barrier, inc=1, device_id=peer, device_id_type=MESH)
    arriving = [
        pltpu.make_async_copy(source, target, in_sem.at[place])
        for place, (source, target) in enumerate(zip(sources, inputs))
    ]
    early = (3, 4, 7, 8, 9)
    late = [place for place in range(1, len(inputs)) if place not in early]
    for place in (*early, 0, *late):
        arriving[place].start()

    def spread(slots, own, peers, send_sem, recv_sem):
        for peer in peers:
            pltpu.make_async_remote_copy(
                src_ref=slots.at[own],
                dst_ref=slots.at[own],
                send_sem=send_sem,
                recv_sem=recv_sem,
                device_id=peer,
                device_id_type=MESH,
            ).start()

    def collect(slots, peers, sem):
        wait_for(slots.at[pl.ds(0, len(peers))], sem)

    def total(slots):
        values = [slots[slot] for slot in range(slots.shape[0])]
        while len(values) > 1:
            values = [
                sum(values[at + 1 : at + 2], values[at]) for at in range(0, len(values), 2)
            ]
        return values[0]

    lane = lax.broadcasted_iota(jnp.int32, (1, LANES), 1)
    leaves = lax.rem(lane, 2 * WIDTH) < WIDTH

    for place in early:
        arriving[place].wait()
    for dest in range(size_r):
        tile = (dest * WIDTH) // LANES * LANES
        place = (dest * WIDTH) % LANES

        def placed(row, first):
            low = pltpu.roll(row, (first - place) % LANES, 1)
            high = pltpu.roll(row, (first + 2 * WIDTH - place) % LANES, 1)
            return jnp.where(lane < 2 * WIDTH, low, high)

        begins = cross_ends[0, :, tile : tile + LANES].astype(F32)
        finish = cross_ends[1, :, tile : tile + LANES].astype(F32)
        used = lax.rem(lane, WIDTH) < counts[0:1, dest : dest + 1]
        bound = jnp.where(used, cross_limit[0:1, tile : tile + LANES], 0.0)
        block = slice(dest * LANES, (dest + 1) * LANES)
        ends_row[:, block] = placed(begins, 0)
        far_row[:, block] = placed(finish, 0)
        bound_row[:, block] = placed(bound, 0)
        info_out[dest, 0:1] = placed(finish, WIDTH)
        info_out[dest, 1:2] = placed(bound, WIDTH)
        info_out[dest, 2:3] = placed(begins, WIDTH)
        info_out[dest, 3:4] = jnp.zeros((1, LANES), F32)
    info_in[r] = jnp.zeros(info_in.shape[1:], F32)
    raw[r] = jnp.zeros(raw.shape[1:], F32)

    pad_row[...] = jnp.zeros((1, LANES), F32)
    owned = cost.shape[1]
    pad_row[:, 0:owned] = cost[...]
    per_tile = LANES // owned
    tile = pl.multiple_of(lax.div(h, per_tile) * LANES, LANES)
    cols = owner[0:1, pl.ds(tile, LANES)]
    where_in = lax.rem(h, per_tile)
    mine = cols
    for place in range(1, per_tile):
        moved = pltpu.roll(cols, (LANES - place * owned) % LANES, 1)
        mine = jnp.where(where_in == place, moved, mine)
    mine = jnp.where(lane < owned, mine, -1)
    col_tech = jnp.where(mine < 0, -1, lax.shift_right_arithmetic(mine, 7))
    col_node = jnp.where(mine < 0, -1, lax.rem(mine, nodes))
    node_iota = lax.broadcasted_iota(jnp.int32, (nodes, LANES), 0)
    tech_iota = lax.broadcasted_iota(jnp.int32, (tech, LANES), 0)
    col_hot = jnp.where(col_node == node_iota, 1.0, 0.0).astype(BF16)
    tech_hot = jnp.where(col_tech == tech_iota, 1.0, 0.0)
    start_a[in_a, tech:] = times_transposed(tech_hot * pad_row[...], col_hot)

    arriving[0].wait()
    weights = zero = jnp.zeros((tech, nodes), F32)
    for at in range(0, rows, 8):
        weights = weights + jnp.sum(avail[at : at + 8], axis=0)
    start_a[in_a, :tech] = weights

    pl.semaphore_wait(barrier, len(everyone))
    spread(start_a, in_a, peers_a, start_send.at[0], start_recv.at[0])
    for j in range(1, size_r):
        dest = lax.rem(r + j, size_r)
        pltpu.make_async_remote_copy(
            src_ref=info_out.at[dest],
            dst_ref=info_in.at[r],
            send_sem=info_send,
            recv_sem=info_recv,
            device_id=device(h, dest),
            device_id_type=MESH,
        ).start()
    for peer in peers_r:
        pltpu.make_async_remote_copy(
            src_ref=sources[13],
            dst_ref=raw.at[r],
            send_sem=raw_send,
            recv_sem=raw_recv,
            device_id=peer,
            device_id_type=MESH,
        ).start()
    for place in late:
        arriving[place].wait()

    lines = line_limit.shape[1]
    units = energy.shape[1]
    line_iota = lax.broadcasted_iota(jnp.int32, (nodes, lines), 0)
    local[:, :lines] = (
        jnp.where(line_ends[1:2] == line_iota, 1.0, 0.0)
        - jnp.where(line_ends[0:1] == line_iota, 1.0, 0.0)
    ).astype(BF16)
    local[:, lines:] = jnp.where(store_node[...] == line_iota, 1.0, 0.0).astype(BF16)
    local_gaps = times(price_start[...], local[...])

    def first_dispatch(i, primal):
        here = pl.ds(i * 8, 8)
        new = jnp.maximum(-0.5 * (gen[...] + price_start[here][:, None, :]), 0.0)
        disp[here] = new
        bal[here] = jnp.sum(new + new, axis=1) - demand[here]
        return primal + jnp.sum(new * new, axis=0)

    primal = lax.fori_loop(0, rows // 8, first_dispatch, zero, unroll=True)

    collect(start_a, peers_a, start_recv.at[0])
    start_b[in_b] = total(start_a)
    spread(start_b, in_b, peers_b, start_send.at[1], start_recv.at[1])

    collect(info_in, peers_r, info_recv)
    for dest in range(size_r):
        block = slice(dest * LANES, (dest + 1) * LANES)
        near_at = jnp.where(leaves, ends_row[:, block], info_in[dest, 0:1]).astype(jnp.int32)
        far_at = jnp.where(leaves, far_row[:, block], info_in[dest, 2:3]).astype(jnp.int32)
        bound_row[:, block] = jnp.where(leaves, bound_row[:, block], info_in[dest, 1:2])
        sign = jnp.where(leaves, -1.0, 1.0)
        hot = jnp.where(near_at == node_iota, sign, 0.0)
        wide[:nodes, block] = jnp.where(lane < 2 * WIDTH, hot, 0.0).astype(BF16)
        wide[nodes:, block] = jnp.where(lane < 2 * WIDTH, 0.0, hot).astype(BF16)
        hot = jnp.where(far_at == node_iota, -sign, 0.0)
        wide_far[:nodes, block] = jnp.where(lane < 2 * WIDTH, hot, 0.0).astype(BF16)
        wide_far[nodes:, block] = jnp.where(lane < 2 * WIDTH, 0.0, hot).astype(BF16)

    def packed(values):
        return jnp.concatenate([values[:half], values[half:]], axis=1)

    near = times(packed(price_start[...]), wide[...])
    collect(raw, peers_r, raw_recv)
    gaps = near + jnp.concatenate(
        [
            times(packed(raw[dest]), wide_far[:, dest * LANES : (dest + 1) * LANES])
            for dest in range(size_r)
        ],
        axis=1,
    )

    def send_duals(phase, values):
        near = times(packed(values), wide[...])
        for dest in range(size_r):
            msg[phase, dest] = near[:, dest * LANES : (dest + 1) * LANES]
        far[phase, r] = jnp.zeros((half, LANES), F32)
        for j in range(1, size_r):
            dest = lax.rem(r + j, size_r)
            pltpu.make_async_remote_copy(
                src_ref=msg.at[phase, dest],
                dst_ref=far.at[phase, r],
                send_sem=msg_send.at[phase],
                recv_sem=msg_recv.at[phase],
                device_id=device(h, dest),
                device_id_type=MESH,
            ).start()

    def slot_gaps(phase):
        collect(far.at[phase], peers_r, msg_recv.at[phase])
        gaps = []
        for dest in range(size_r):
            block = far[phase, dest]
            swapped = jnp.where(
                leaves, pltpu.roll(block, LANES - WIDTH, 1), pltpu.roll(block, WIDTH, 1)
            )
            gaps.append(swapped + msg[phase, dest])
        return jnp.concatenate(gaps, axis=1)

    capacity = zero
    pull = zero
    last_charge = jnp.zeros((1, units), F32)
    next_dual = jnp.zeros((1, units), F32)
    prev_dual = jnp.zeros((1, units), F32)
    weight = jnp.ones((1, 1), F32)
    unit_rows = lax.broadcasted_iota(jnp.int32, (rows, units), 0)
    cross_old = jnp.zeros(cross.shape, F32)
    inner_old = jnp.zeros(inner.shape, F32)
    dis_old = jnp.zeros(discharge.shape, F32)
    charge_old = jnp.zeros(charge.shape, F32)
    sd_old = jnp.zeros(sdual.shape, F32)
    price_old = price_start[...]

    for iteration in range(ITERS):
        start = iteration == 0
        final = iteration == ITERS - 1
        step = 0.5 / weight
        gap_line, gap_unit = local_gaps[:, :lines], local_gaps[:, lines:]
        bounds = bound_row[...]
        limit = line_limit[...]
        if not start:
            cross_old = cross[...]
            inner_old = inner[...]
            dis_old = discharge[...]
            charge_old = charge[...]
            sd_old = sdual[...]
            price_old = prices[...]
        cross_new = jnp.clip(cross_old - step * gaps, -bounds, bounds)
        inner_new = jnp.clip(inner_old - step * gap_line, -limit, limit)
        dis_new = jnp.clip(dis_old - step * (gap_unit + sd_old), -power[...], power[...])
        sd_next = jnp.where(
            unit_rows == rows - 1, next_dual, pltpu.roll(sd_old, rows - 1, 0)
        )
        charge_new = jnp.clip(charge_old - step * (sd_old - sd_next), 0.0, energy[...])
        cross_gain = cross_new - cross_old
        inner_gain = inner_new - inner_old
        dis_gain = dis_new - dis_old
        dis_bar = dis_new + dis_gain
        charge[...] = charge_new
        net = times_transposed(cross_new + cross_gain, wide[...])
        flow = jnp.concatenate([inner_new + inner_gain, dis_bar], axis=1)
        moved = jnp.concatenate(
            [net[:, :nodes], net[:, nodes:]], axis=0
        ) + times_transposed(flow, local[...])
        step_b = jnp.broadcast_to(step, (tech, nodes))

        def new_capacity():
            return jnp.maximum(capacity - (col_cost - pull) / (weight * col_weight), 0.0)

        if final:
            capacity = new_capacity()
            picked = times(capacity, col_hot) * tech_hot
            cap_row[...] = jnp.sum(picked, axis=0, keepdims=True)[:, :owned]

            def last_hours(i, carry):
                here = pl.ds(i * 8, 8)
                old = disp[here]
                new = jnp.maximum(old - step_b * slope[here], 0.0)
                bal[here] = jnp.sum(new + (new - old), axis=1) - demand[here]
                disp[here] = new
                return carry

            lax.fori_loop(0, rows // 8, last_hours, 0, unroll=True)
            prices[...] = price_old + weight / (tech + 8.0) * (bal[...] + moved)
            break

        charge_gain = charge_new - charge_old
        charge_bar = charge_new + charge_gain
        last_new = jnp.clip(last_charge - step * (prev_dual - sd_old[0:1]), 0.0, energy[...])
        last_bar = last_new + (last_new - last_charge)
        last_charge = last_new
        before = jnp.where(unit_rows == 0, last_bar, pltpu.roll(charge_bar, 1, 0))
        sd_gain = weight / 3.0 * (charge_bar - before + dis_bar)
        sd_new = sd_old + sd_gain
        sd_step = sd_new - sd_old
        primal_row = (
            fold(inner_gain * inner_gain)
            + fold(cross_gain * cross_gain) * jnp.where(leaves, 1.0, 0.0)
            + fold(dis_gain * dis_gain)
            + fold(charge_gain * charge_gain)
        )
        dual_row = fold(sd_step * sd_step)

        half_weight = jnp.broadcast_to(weight / 2.0, (tech, nodes))
        if start:
            price_new = price_old + weight / (tech + 8.0) * (bal[...] + moved)
            send_duals(1, price_new)
            price_gain = price_new - price_old
            primal_row += fold(primal)
            dual_row += fold(price_gain * price_gain)
            collect(start_b, peers_b, start_recv.at[1])
            both = total(start_b)
            col_weight, col_cost = both[:tech], both[tech:]
            cap_new = new_capacity()
            cap_gain = cap_new - capacity
            cap_bar = cap_new + cap_gain

            def first_duals(i, dual):
                here = pl.ds(i * 8, 8)
                new = disp[here]
                dual_new = jnp.maximum(
                    half_weight * (new + new - avail[here] * cap_bar), 0.0
                )
                capd[here] = dual_new
                return dual + jnp.sum(dual_new * dual_new, axis=0)

            dual = lax.fori_loop(0, rows // 8, first_duals, zero, unroll=True)
        else:
            cap_new = new_capacity()
            cap_gain = cap_new - capacity
            cap_bar = cap_new + cap_gain

            def some_hours(i, carry):
                primal, dual = carry
                here = pl.ds(i * 8, 8)
                old = disp[here]
                dual_old = capd[here]
                new = jnp.maximum(old - step_b * slope[here], 0.0)
                gain = new - old
                bar = new + gain
                bal[here] = jnp.sum(bar, axis=1) - demand[here]
                dual_new = jnp.maximum(
                    dual_old + half_weight * (bar - avail[here] * cap_bar), 0.0
                )
                dual_gain = dual_new - dual_old
                disp[here] = new
                capd[here] = dual_new
                return (
                    primal + jnp.sum(gain * gain, axis=0),
                    dual + jnp.sum(dual_gain * dual_gain, axis=0),
                )

            primal, dual = lax.fori_loop(0, rows // 8, some_hours, (zero, zero), unroll=True)
            price_new = price_old + weight / (tech + 8.0) * (bal[...] + moved)
            price_gain = price_new - price_old
            primal_row += fold(primal)
            dual_row += fold(price_gain * price_gain)

        capacity = cap_new
        primal_row += fold(cap_gain * cap_gain) * (1.0 / hours)
        dual_row += fold(dual)
        in_zx = in_b * size_x + in_x
        sq_a[iteration, in_zx, 0:1] = primal_row
        sq_a[iteration, in_zx, 1:2] = dual_row
        spread(
            sq_a.at[iteration],
            in_zx,
            peers_zx,
            sq_send.at[iteration, 0],
            sq_recv.at[iteration, 0],
        )

        cross[...] = cross_new
        inner[...] = inner_new
        discharge[...] = dis_new
        sdual[...] = sd_new
        prices[...] = price_new

        def prepare(i, pull_sum):
            here = pl.ds(i * 8, 8)
            dual_now = capd[here]
            slope[here] = gen[...] + prices[here][:, None, :] + dual_now
            return pull_sum + jnp.sum(avail[here] * dual_now, axis=0)

        col_a[iteration, in_a] = lax.fori_loop(0, rows // 8, prepare, zero, unroll=True)
        spread(
            col_a.at[iteration],
            in_a,
            peers_a,
            col_send.at[iteration, 0],
            col_recv.at[iteration, 0],
        )
        halo_out[iteration, 0] = sd_new[0:1]
        halo_out[iteration, 1] = sd_new[rows - 1 : rows]
        for side, peer in ((0, preceding), (1, following)):
            pltpu.make_async_remote_copy(
                src_ref=halo_out.at[iteration, side],
                dst_ref=halo_in.at[iteration, side],
                send_sem=halo_send.at[iteration, side],
                recv_sem=halo_recv.at[iteration, side],
                device_id=peer,
                device_id_type=MESH,
            ).start()
        if not start:
            send_duals(iteration + 1, price_new)
        local_gaps = times(price_new, local[...])

        collect(col_a.at[iteration], peers_a, col_recv.at[iteration, 0])
        col_b[iteration, in_b] = total(col_a.at[iteration])
        spread(
            col_b.at[iteration],
            in_b,
            peers_b,
            col_send.at[iteration, 1],
            col_recv.at[iteration, 1],
        )
        collect(sq_a.at[iteration], peers_zx, sq_recv.at[iteration, 0])
        in_rc = r * cores + core
        sq_b[iteration, in_rc] = total(sq_a.at[iteration])
        spread(
            sq_b.at[iteration],
            in_rc,
            peers_rc,
            sq_send.at[iteration, 1],
            sq_recv.at[iteration, 1],
        )
        gaps = slot_gaps(iteration + 1)
        wait_for(halo_in.at[iteration, 0], halo_recv.at[iteration, 0])
        wait_for(halo_in.at[iteration, 1], halo_recv.at[iteration, 1])
        next_dual = halo_in[iteration, 0]
        prev_dual = halo_in[iteration, 1]
        collect(col_b.at[iteration], peers_b, col_recv.at[iteration, 1])
        pull = total(col_b.at[iteration])
        collect(sq_b.at[iteration], peers_rc, sq_recv.at[iteration, 1])
        sums = jnp.sum(total(sq_b.at[iteration]), axis=1, keepdims=True)
        ratio = (sums[1:2] + EPSILON) / (sums[0:1] + EPSILON)
        weight = jnp.sqrt(weight * jnp.sqrt(ratio))

    collect(info_in, peers_r, info_send)
    collect(raw, peers_r, raw_send)
    collect(start_a, peers_a, start_send.at[0])
    collect(start_b, peers_b, start_send.at[1])
    for phase in range(1, ITERS):
        collect(far.at[phase], peers_r, msg_send.at[phase])
    for phase in range(PHASES):
        collect(sq_a.at[phase], peers_zx, sq_send.at[phase, 0])
        collect(sq_b.at[phase], peers_rc, sq_send.at[phase, 1])
        collect(col_a.at[phase], peers_a, col_send.at[phase, 0])
        collect(col_b.at[phase], peers_b, col_send.at[phase, 1])
        for side in range(2):
            wait_for(halo_out.at[phase, side], halo_send.at[phase, side])


def store_outputs(*refs):
    sources, targets, sem = refs[:4], refs[4:8], refs[8]
    copies = [
        pltpu.make_async_copy(source, target, sem.at[place])
        for place, (source, target) in enumerate(zip(sources, targets))
    ]
    for copy in copies:
        copy.start()
    for copy in copies:
        copy.wait()


def body(
    availability,
    demand,
    gen_cost,
    cap_cost,
    owner_map,
    line_ends,
    line_limit,
    cross_ends,
    cross_limit,
    pair_counts,
    store_node,
    store_energy,
    store_power,
    price_start,
):
    rows, tech, nodes = availability.shape
    lines = line_limit.shape[0]
    units = store_node.shape[0]
    regions = lax.axis_size("region")
    hours = lax.axis_size("hours")
    size_a = 8 if hours % 64 == 0 else 2
    size_b = hours // size_a
    half = rows // 2
    slots = regions * LANES
    dma = pltpu.SemaphoreType.DMA
    arrays = (
        availability,
        demand,
        gen_cost,
        cap_cost,
        owner_map,
        line_ends,
        line_limit[None],
        cross_ends,
        cross_limit,
        pair_counts,
        store_node[None],
        store_energy[None],
        store_power[None],
        price_start,
    )
    scratch = [pltpu.VMEM(array.shape, array.dtype) for array in arrays] + [
        dma((len(arrays),)),
        pltpu.VMEM((rows, tech, nodes), F32),
        pltpu.VMEM((rows, tech, nodes), F32),
        pltpu.VMEM((rows, lines), F32),
        pltpu.VMEM((rows, units), F32),
        pltpu.VMEM((rows, units), F32),
        pltpu.VMEM((half, slots), F32),
        pltpu.VMEM((rows, nodes), F32),
        pltpu.VMEM((2 * nodes, slots), BF16),
        pltpu.VMEM((2 * nodes, slots), BF16),
        pltpu.VMEM((nodes, lines + units), BF16),
        pltpu.VMEM((1, slots), F32),
        pltpu.VMEM((1, slots), F32),
        pltpu.VMEM((1, slots), F32),
        pltpu.VMEM((regions, rows, nodes), F32),
        pltpu.VMEM((ITERS, regions, half, LANES), F32),
        pltpu.VMEM((ITERS, regions, half, LANES), F32),
        pltpu.VMEM((regions, 4, LANES), F32),
        pltpu.VMEM((regions, 4, LANES), F32),
        pltpu.VMEM((size_a, 2 * tech, nodes), F32),
        pltpu.VMEM((size_b, 2 * tech, nodes), F32),
        pltpu.VMEM((PHASES, size_a, tech, nodes), F32),
        pltpu.VMEM((PHASES, size_b, tech, nodes), F32),
        pltpu.VMEM((PHASES, hours // 2, 2, LANES), F32),
        pltpu.VMEM((PHASES, 2 * regions, 2, LANES), F32),
        pltpu.VMEM((PHASES, 2, 1, units), F32),
        pltpu.VMEM((PHASES, 2, 1, units), F32),
        pltpu.VMEM((1, LANES), F32),
        dma(()),
        dma(()),
        dma((ITERS,)),
        dma((ITERS,)),
        dma(()),
        dma(()),
        dma((2,)),
        dma((2,)),
        dma((PHASES, 2)),
        dma((PHASES, 2)),
        dma((PHASES, 2)),
        dma((PHASES, 2)),
        dma((PHASES, 2)),
        dma((PHASES, 2)),
    ]
    hbm = pl.BlockSpec(memory_space=pltpu.HBM)
    vmem = pl.BlockSpec(memory_space=pltpu.VMEM)
    outs = pl.pallas_call(
        functools.partial(kernel, (size_a // 2, size_b, regions)),
        out_shape=(
            pltpu.VMEM((rows, tech, nodes), F32),
            pltpu.VMEM(cap_cost.shape, F32),
            pltpu.VMEM((rows, nodes), F32),
            pltpu.VMEM((rows, units), F32),
        ),
        in_specs=[hbm] * len(arrays),
        out_specs=(vmem,) * 4,
        scratch_shapes=scratch,
        compiler_params=pltpu.CompilerParams(
            collective_id=0, has_side_effects=True, vmem_limit_bytes=60 * 1024 * 1024
        ),
    )(*arrays)
    return pl.pallas_call(
        store_outputs,
        out_shape=tuple(jax.ShapeDtypeStruct(out.shape, F32) for out in outs),
        in_specs=[vmem] * 4,
        out_specs=(hbm,) * 4,
        scratch_shapes=[dma((4,))],
        compiler_params=pltpu.CompilerParams(vmem_limit_bytes=4 * 1024 * 1024),
    )(*outs)


def solution(mesh):
    placed = (
        P("hours", None, "region"),
        P("hours", "region"),
        P(None, "region"),
        P("region", "hours"),
        P("region", None),
        P(None, "region"),
        P("region"),
        P(None, "region", None),
        P("region", None),
        P("region", None),
        P("region"),
        P("region"),
        P("region"),
        P("hours", "region"),
    )
    return jax.shard_map(
        body,
        mesh=mesh,
        in_specs=placed,
        out_specs=(
            P("hours", None, "region"),
            P("region", "hours"),
            P("hours", "region"),
            P("hours", "region"),
        ),
        check_vma=False,
    )
```

```python
import functools

import jax
import jax.numpy as jnp
from jax import lax
from jax.experimental import pallas as pl
from jax.experimental.pallas import tpu as pltpu
from jax.sharding import PartitionSpec as P

ITERS = 4
PHASES = ITERS - 1
EPSILON = 1e-06
LANES = 128
WIDTH = 32
PARTS = 2
F32 = jnp.float32
BF16 = jnp.bfloat16
MESH = pl.DeviceIdType.MESH


def split(value, parts=PARTS):
    pieces = []
    for part in range(parts):
        piece = value.astype(BF16)
        pieces.append(piece)
        if part + 1 < parts:
            value = value - piece.astype(F32)
    return jnp.concatenate(pieces, axis=0)


def joined(value, parts=PARTS):
    rows = value.shape[0] // parts
    total = value[(parts - 1) * rows :]
    for part in range(parts - 2, -1, -1):
        total = total + value[part * rows : (part + 1) * rows]
    return total


def times(value, matrix):
    product = jnp.dot(split(value), matrix, preferred_element_type=F32)
    return joined(product)


def times_transposed(value, matrix):
    product = lax.dot_general(
        split(value), matrix, (((1,), (1,)), ((), ())), preferred_element_type=F32
    )
    return joined(product)


def fold(value):
    rows, cols = value.shape
    total = value[:, :LANES]
    for tile in range(1, cols // LANES):
        total = total + value[:, tile * LANES : (tile + 1) * LANES]
    if rows > 8:
        total = jnp.sum(total.reshape(rows // 8, 8, LANES), axis=0)
    return jnp.sum(total, axis=0, keepdims=True)


def wait_for(ref, sem):
    pltpu.make_async_copy(ref, ref, sem).wait()


def kernel(groups, *refs):
    sources, results, inputs = refs[:14], refs[14:18], refs[18:32]
    steps(groups, sources, inputs, results, *inputs, *refs[32:])


def steps(
    groups,
    sources,
    inputs,
    results,
    avail,
    demand,
    gen,
    cost,
    owner,
    line_ends,
    line_limit,
    cross_ends,
    cross_limit,
    counts,
    store_node,
    energy,
    power,
    price_start,
    in_sem,
    capd,
    slope,
    inner,
    discharge,
    sdual,
    cross,
    bal,
    wide,
    wide_far,
    local,
    ends_row,
    far_row,
    bound_row,
    raw,
    msg,
    far,
    info_out,
    info_in,
    start_a,
    start_b,
    col_a,
    col_b,
    sq_a,
    sq_b,
    halo_out,
    halo_in,
    pad_row,
    raw_send,
    raw_recv,
    msg_send,
    msg_recv,
    info_send,
    info_recv,
    start_send,
    start_recv,
    col_send,
    col_recv,
    sq_send,
    sq_recv,
    halo_send,
    halo_recv,
):
    size_x, size_z, size_r = groups
    disp, cap_row, prices, charge = results
    cores = 2
    size_a, size_b = size_x * cores, size_z
    hours = size_a * size_b
    rows, tech, nodes = avail.shape
    half = rows // 2
    h = lax.axis_index("hours")
    r = lax.axis_index("region")
    core = lax.rem(h, cores)
    in_a = lax.rem(h, size_a)
    in_x = lax.div(in_a, cores)
    in_b = lax.div(h, size_a)

    def device(hour, region):
        return {"hours": hour, "region": region}

    def others(first, second):
        def hops(step):
            return min(step[0], first - step[0]) + min(step[1], second - step[1])

        pairs = [(i, j) for i in range(first) for j in range(second) if i or j]
        return sorted(pairs, key=hops, reverse=True)

    peers_a = [
        device(in_b * size_a + lax.rem(in_a + j, size_a), r) for j in range(1, size_a)
    ]
    peers_b = [
        device(lax.rem(in_b + j, size_b) * size_a + in_a, r) for j in range(1, size_b)
    ]
    peers_r = [device(h, lax.rem(r + j, size_r)) for j in range(1, size_r)]
    peers_zx = [
        device(
            lax.rem(in_b + i, size_z) * size_a + lax.rem(in_x + j, size_x) * cores + core, r
        )
        for i, j in others(size_z, size_x)
    ]
    peers_rc = [
        device(h - core + lax.rem(core + j, cores), lax.rem(r + i, size_r))
        for i, j in others(size_r, cores)
    ]
    following = device(lax.rem(h + 1, hours), r)
    preceding = device(lax.rem(h + hours - 1, hours), r)

    barrier = pltpu.get_barrier_semaphore()
    everyone = peers_b + peers_rc + peers_a
    for peer in everyone:
        pl.semaphore_signal(barrier, inc=1, device_id=peer, device_id_type=MESH)
    arriving = [
        pltpu.make_async_copy(source, target, in_sem.at[place])
        for place, (source, target) in enumerate(zip(sources, inputs))
    ]
    early = (3, 4, 7, 8, 9)
    late = [place for place in range(1, len(inputs)) if place not in early]
    for place in (*early, 0, *late):
        arriving[place].start()

    def spread(slots, own, peers, send_sem, recv_sem):
        for peer in peers:
            pltpu.make_async_remote_copy(
                src_ref=slots.at[own],
                dst_ref=slots.at[own],
                send_sem=send_sem,
                recv_sem=recv_sem,
                device_id=peer,
                device_id_type=MESH,
            ).start()

    def collect(slots, peers, sem):
        wait_for(slots.at[pl.ds(0, len(peers))], sem)

    def total(slots):
        values = [slots[slot] for slot in range(slots.shape[0])]
        while len(values) > 1:
            values = [
                sum(values[at + 1 : at + 2], values[at]) for at in range(0, len(values), 2)
            ]
        return values[0]

    lane = lax.broadcasted_iota(jnp.int32, (1, LANES), 1)
    leaves = lax.rem(lane, 2 * WIDTH) < WIDTH

    for place in early:
        arriving[place].wait()
    for dest in range(size_r):
        tile = (dest * WIDTH) // LANES * LANES
        place = (dest * WIDTH) % LANES

        def placed(row, first):
            low = pltpu.roll(row, (first - place) % LANES, 1)
            high = pltpu.roll(row, (first + 2 * WIDTH - place) % LANES, 1)
            return jnp.where(lane < 2 * WIDTH, low, high)

        begins = cross_ends[0, :, tile : tile + LANES].astype(F32)
        finish = cross_ends[1, :, tile : tile + LANES].astype(F32)
        used = lax.rem(lane, WIDTH) < counts[0:1, dest : dest + 1]
        bound = jnp.where(used, cross_limit[0:1, tile : tile + LANES], 0.0)
        block = slice(dest * LANES, (dest + 1) * LANES)
        ends_row[:, block] = placed(begins, 0)
        far_row[:, block] = placed(finish, 0)
        bound_row[:, block] = placed(bound, 0)
        info_out[dest, 0:1] = placed(finish, WIDTH)
        info_out[dest, 1:2] = placed(bound, WIDTH)
        info_out[dest, 2:3] = placed(begins, WIDTH)
        info_out[dest, 3:4] = jnp.zeros((1, LANES), F32)
    info_in[r] = jnp.zeros(info_in.shape[1:], F32)
    raw[r] = jnp.zeros(raw.shape[1:], F32)

    pad_row[...] = jnp.zeros((1, LANES), F32)
    owned = cost.shape[1]
    pad_row[:, 0:owned] = cost[...]
    per_tile = LANES // owned
    tile = pl.multiple_of(lax.div(h, per_tile) * LANES, LANES)
    cols = owner[0:1, pl.ds(tile, LANES)]
    where_in = lax.rem(h, per_tile)
    mine = cols
    for place in range(1, per_tile):
        moved = pltpu.roll(cols, (LANES - place * owned) % LANES, 1)
        mine = jnp.where(where_in == place, moved, mine)
    mine = jnp.where(lane < owned, mine, -1)
    col_tech = jnp.where(mine < 0, -1, lax.shift_right_arithmetic(mine, 7))
    col_node = jnp.where(mine < 0, -1, lax.rem(mine, nodes))
    node_iota = lax.broadcasted_iota(jnp.int32, (nodes, LANES), 0)
    tech_iota = lax.broadcasted_iota(jnp.int32, (tech, LANES), 0)
    col_hot = jnp.where(col_node == node_iota, 1.0, 0.0).astype(BF16)
    tech_hot = jnp.where(col_tech == tech_iota, 1.0, 0.0)
    start_a[in_a, tech:] = times_transposed(tech_hot * pad_row[...], col_hot)

    arriving[0].wait()
    weights = zero = jnp.zeros((tech, nodes), F32)
    for at in range(0, rows, 8):
        weights = weights + jnp.sum(avail[at : at + 8], axis=0)
    start_a[in_a, :tech] = weights

    pl.semaphore_wait(barrier, len(everyone))
    spread(start_a, in_a, peers_a, start_send.at[0], start_recv.at[0])
    for j in range(1, size_r):
        dest = lax.rem(r + j, size_r)
        pltpu.make_async_remote_copy(
            src_ref=info_out.at[dest],
            dst_ref=info_in.at[r],
            send_sem=info_send,
            recv_sem=info_recv,
            device_id=device(h, dest),
            device_id_type=MESH,
        ).start()
    for peer in peers_r:
        pltpu.make_async_remote_copy(
            src_ref=sources[13],
            dst_ref=raw.at[r],
            send_sem=raw_send,
            recv_sem=raw_recv,
            device_id=peer,
            device_id_type=MESH,
        ).start()
    for place in late:
        arriving[place].wait()

    lines = line_limit.shape[1]
    units = energy.shape[1]
    line_iota = lax.broadcasted_iota(jnp.int32, (nodes, lines), 0)
    local[:, :lines] = (
        jnp.where(line_ends[1:2] == line_iota, 1.0, 0.0)
        - jnp.where(line_ends[0:1] == line_iota, 1.0, 0.0)
    ).astype(BF16)
    local[:, lines:] = jnp.where(store_node[...] == line_iota, 1.0, 0.0).astype(BF16)
    local_gaps = times(price_start[...], local[...])

    def first_dispatch(i, primal):
        here = pl.ds(i * 8, 8)
        new = jnp.maximum(-0.5 * (gen[...] + price_start[here][:, None, :]), 0.0)
        disp[here] = new
        bal[here] = jnp.sum(new + new, axis=1) - demand[here]
        return primal + jnp.sum(new * new, axis=0)

    primal = lax.fori_loop(0, rows // 8, first_dispatch, zero, unroll=True)

    collect(start_a, peers_a, start_recv.at[0])
    start_b[in_b] = total(start_a)
    spread(start_b, in_b, peers_b, start_send.at[1], start_recv.at[1])

    collect(info_in, peers_r, info_recv)
    for dest in range(size_r):
        block = slice(dest * LANES, (dest + 1) * LANES)
        near_at = jnp.where(leaves, ends_row[:, block], info_in[dest, 0:1]).astype(jnp.int32)
        far_at = jnp.where(leaves, far_row[:, block], info_in[dest, 2:3]).astype(jnp.int32)
        bound_row[:, block] = jnp.where(leaves, bound_row[:, block], info_in[dest, 1:2])
        sign = jnp.where(leaves, -1.0, 1.0)
        hot = jnp.where(near_at == node_iota, sign, 0.0)
        wide[:nodes, block] = jnp.where(lane < 2 * WIDTH, hot, 0.0).astype(BF16)
        wide[nodes:, block] = jnp.where(lane < 2 * WIDTH, 0.0, hot).astype(BF16)
        hot = jnp.where(far_at == node_iota, -sign, 0.0)
        wide_far[:nodes, block] = jnp.where(lane < 2 * WIDTH, hot, 0.0).astype(BF16)
        wide_far[nodes:, block] = jnp.where(lane < 2 * WIDTH, 0.0, hot).astype(BF16)

    def packed(values):
        return jnp.concatenate([values[:half], values[half:]], axis=1)

    near = times(packed(price_start[...]), wide[...])
    collect(raw, peers_r, raw_recv)
    gaps = near + jnp.concatenate(
        [
            times(packed(raw[dest]), wide_far[:, dest * LANES : (dest + 1) * LANES])
            for dest in range(size_r)
        ],
        axis=1,
    )

    def send_duals(phase, values):
        near = times(packed(values), wide[...])
        for dest in range(size_r):
            msg[phase, dest] = near[:, dest * LANES : (dest + 1) * LANES]
        far[phase, r] = jnp.zeros((half, LANES), F32)
        for j in range(1, size_r):
            dest = lax.rem(r + j, size_r)
            pltpu.make_async_remote_copy(
                src_ref=msg.at[phase, dest],
                dst_ref=far.at[phase, r],
                send_sem=msg_send.at[phase],
                recv_sem=msg_recv.at[phase],
                device_id=device(h, dest),
                device_id_type=MESH,
            ).start()

    def slot_gaps(phase):
        collect(far.at[phase], peers_r, msg_recv.at[phase])
        gaps = []
        for dest in range(size_r):
            block = far[phase, dest]
            swapped = jnp.where(
                leaves, pltpu.roll(block, LANES - WIDTH, 1), pltpu.roll(block, WIDTH, 1)
            )
            gaps.append(swapped + msg[phase, dest])
        return jnp.concatenate(gaps, axis=1)

    capacity = zero
    pull = zero
    last_charge = jnp.zeros((1, units), F32)
    next_dual = jnp.zeros((1, units), F32)
    prev_dual = jnp.zeros((1, units), F32)
    weight = jnp.ones((1, 1), F32)
    unit_rows = lax.broadcasted_iota(jnp.int32, (rows, units), 0)
    cross_old = jnp.zeros(cross.shape, F32)
    inner_old = jnp.zeros(inner.shape, F32)
    dis_old = jnp.zeros(discharge.shape, F32)
    charge_old = jnp.zeros(charge.shape, F32)
    sd_old = jnp.zeros(sdual.shape, F32)
    price_old = price_start[...]

    for iteration in range(ITERS):
        start = iteration == 0
        final = iteration == ITERS - 1
        step = 0.5 / weight
        gap_line, gap_unit = local_gaps[:, :lines], local_gaps[:, lines:]
        bounds = bound_row[...]
        limit = line_limit[...]
        if not start:
            cross_old = cross[...]
            inner_old = inner[...]
            dis_old = discharge[...]
            charge_old = charge[...]
            sd_old = sdual[...]
            price_old = prices[...]
        cross_new = jnp.clip(cross_old - step * gaps, -bounds, bounds)
        inner_new = jnp.clip(inner_old - step * gap_line, -limit, limit)
        dis_new = jnp.clip(dis_old - step * (gap_unit + sd_old), -power[...], power[...])
        sd_next = jnp.where(
            unit_rows == rows - 1, next_dual, pltpu.roll(sd_old, rows - 1, 0)
        )
        charge_new = jnp.clip(charge_old - step * (sd_old - sd_next), 0.0, energy[...])
        cross_gain = cross_new - cross_old
        inner_gain = inner_new - inner_old
        dis_gain = dis_new - dis_old
        dis_bar = dis_new + dis_gain
        charge[...] = charge_new
        net = times_transposed(cross_new + cross_gain, wide[...])
        flow = jnp.concatenate([inner_new + inner_gain, dis_bar], axis=1)
        moved = jnp.concatenate(
            [net[:, :nodes], net[:, nodes:]], axis=0
        ) + times_transposed(flow, local[...])
        step_b = jnp.broadcast_to(step, (tech, nodes))

        def new_capacity():
            return jnp.maximum(capacity - (col_cost - pull) / (weight * col_weight), 0.0)

        if final:
            capacity = new_capacity()
            picked = times(capacity, col_hot) * tech_hot
            cap_row[...] = jnp.sum(picked, axis=0, keepdims=True)[:, :owned]

            def last_hours(i, carry):
                here = pl.ds(i * 8, 8)
                old = disp[here]
                new = jnp.maximum(old - step_b * slope[here], 0.0)
                bal[here] = jnp.sum(new + (new - old), axis=1) - demand[here]
                disp[here] = new
                return carry

            lax.fori_loop(0, rows // 8, last_hours, 0, unroll=True)
            prices[...] = price_old + weight / (tech + 8.0) * (bal[...] + moved)
            break

        charge_gain = charge_new - charge_old
        charge_bar = charge_new + charge_gain
        last_new = jnp.clip(last_charge - step * (prev_dual - sd_old[0:1]), 0.0, energy[...])
        last_bar = last_new + (last_new - last_charge)
        last_charge = last_new
        before = jnp.where(unit_rows == 0, last_bar, pltpu.roll(charge_bar, 1, 0))
        sd_gain = weight / 3.0 * (charge_bar - before + dis_bar)
        sd_new = sd_old + sd_gain
        sd_step = sd_new - sd_old
        primal_row = (
            fold(inner_gain * inner_gain)
            + fold(cross_gain * cross_gain) * jnp.where(leaves, 1.0, 0.0)
            + fold(dis_gain * dis_gain)
            + fold(charge_gain * charge_gain)
        )
        dual_row = fold(sd_step * sd_step)

        half_weight = jnp.broadcast_to(weight / 2.0, (tech, nodes))
        if start:
            price_new = price_old + weight / (tech + 8.0) * (bal[...] + moved)
            send_duals(1, price_new)
            price_gain = price_new - price_old
            primal_row += fold(primal)
            dual_row += fold(price_gain * price_gain)
            collect(start_b, peers_b, start_recv.at[1])
            both = total(start_b)
            col_weight, col_cost = both[:tech], both[tech:]
            cap_new = new_capacity()
            cap_gain = cap_new - capacity
            cap_bar = cap_new + cap_gain

            def first_duals(i, dual):
                here = pl.ds(i * 8, 8)
                new = disp[here]
                dual_new = jnp.maximum(
                    half_weight * (new + new - avail[here] * cap_bar), 0.0
                )
                capd[here] = dual_new
                return dual + jnp.sum(dual_new * dual_new, axis=0)

            dual = lax.fori_loop(0, rows // 8, first_duals, zero, unroll=True)
        else:
            cap_new = new_capacity()
            cap_gain = cap_new - capacity
            cap_bar = cap_new + cap_gain

            def some_hours(i, carry):
                primal, dual = carry
                here = pl.ds(i * 8, 8)
                old = disp[here]
                dual_old = capd[here]
                new = jnp.maximum(old - step_b * slope[here], 0.0)
                gain = new - old
                bar = new + gain
                bal[here] = jnp.sum(bar, axis=1) - demand[here]
                dual_new = jnp.maximum(
                    dual_old + half_weight * (bar - avail[here] * cap_bar), 0.0
                )
                dual_gain = dual_new - dual_old
                disp[here] = new
                capd[here] = dual_new
                return (
                    primal + jnp.sum(gain * gain, axis=0),
                    dual + jnp.sum(dual_gain * dual_gain, axis=0),
                )

            primal, dual = lax.fori_loop(0, rows // 8, some_hours, (zero, zero), unroll=True)
            price_new = price_old + weight / (tech + 8.0) * (bal[...] + moved)
            price_gain = price_new - price_old
            primal_row += fold(primal)
            dual_row += fold(price_gain * price_gain)

        capacity = cap_new
        primal_row += fold(cap_gain * cap_gain) * (1.0 / hours)
        dual_row += fold(dual)
        in_zx = in_b * size_x + in_x
        sq_a[iteration, in_zx, 0:1] = primal_row
        sq_a[iteration, in_zx, 1:2] = dual_row
        spread(
            sq_a.at[iteration],
            in_zx,
            peers_zx,
            sq_send.at[iteration, 0],
            sq_recv.at[iteration, 0],
        )

        cross[...] = cross_new
        inner[...] = inner_new
        discharge[...] = dis_new
        sdual[...] = sd_new
        prices[...] = price_new

        def prepare(i, pull_sum):
            here = pl.ds(i * 8, 8)
            dual_now = capd[here]
            slope[here] = gen[...] + prices[here][:, None, :] + dual_now
            return pull_sum + jnp.sum(avail[here] * dual_now, axis=0)

        col_a[iteration, in_a] = lax.fori_loop(0, rows // 8, prepare, zero, unroll=True)
        spread(
            col_a.at[iteration],
            in_a,
            peers_a,
            col_send.at[iteration, 0],
            col_recv.at[iteration, 0],
        )
        halo_out[iteration, 0] = sd_new[0:1]
        halo_out[iteration, 1] = sd_new[rows - 1 : rows]
        for side, peer in ((0, preceding), (1, following)):
            pltpu.make_async_remote_copy(
                src_ref=halo_out.at[iteration, side],
                dst_ref=halo_in.at[iteration, side],
                send_sem=halo_send.at[iteration, side],
                recv_sem=halo_recv.at[iteration, side],
                device_id=peer,
                device_id_type=MESH,
            ).start()
        if not start:
            send_duals(iteration + 1, price_new)
        local_gaps = times(price_new, local[...])

        collect(col_a.at[iteration], peers_a, col_recv.at[iteration, 0])
        col_b[iteration, in_b] = total(col_a.at[iteration])
        spread(
            col_b.at[iteration],
            in_b,
            peers_b,
            col_send.at[iteration, 1],
            col_recv.at[iteration, 1],
        )
        collect(sq_a.at[iteration], peers_zx, sq_recv.at[iteration, 0])
        in_rc = r * cores + core
        sq_b[iteration, in_rc] = total(sq_a.at[iteration])
        spread(
            sq_b.at[iteration],
            in_rc,
            peers_rc,
            sq_send.at[iteration, 1],
            sq_recv.at[iteration, 1],
        )
        gaps = slot_gaps(iteration + 1)
        wait_for(halo_in.at[iteration, 0], halo_recv.at[iteration, 0])
        wait_for(halo_in.at[iteration, 1], halo_recv.at[iteration, 1])
        next_dual = halo_in[iteration, 0]
        prev_dual = halo_in[iteration, 1]
        collect(col_b.at[iteration], peers_b, col_recv.at[iteration, 1])
        pull = total(col_b.at[iteration])
        collect(sq_b.at[iteration], peers_rc, sq_recv.at[iteration, 1])
        sums = jnp.sum(total(sq_b.at[iteration]), axis=1, keepdims=True)
        ratio = (sums[1:2] + EPSILON) / (sums[0:1] + EPSILON)
        weight = jnp.sqrt(weight * jnp.sqrt(ratio))

    collect(info_in, peers_r, info_send)
    collect(raw, peers_r, raw_send)
    collect(start_a, peers_a, start_send.at[0])
    collect(start_b, peers_b, start_send.at[1])
    for phase in range(1, ITERS):
        collect(far.at[phase], peers_r, msg_send.at[phase])
    for phase in range(PHASES):
        collect(sq_a.at[phase], peers_zx, sq_send.at[phase, 0])
        collect(sq_b.at[phase], peers_rc, sq_send.at[phase, 1])
        collect(col_a.at[phase], peers_a, col_send.at[phase, 0])
        collect(col_b.at[phase], peers_b, col_send.at[phase, 1])
        for side in range(2):
            wait_for(halo_out.at[phase, side], halo_send.at[phase, side])


def store_outputs(*refs):
    sources, targets, sem = refs[:4], refs[4:8], refs[8]
    copies = [
        pltpu.make_async_copy(source, target, sem.at[place])
        for place, (source, target) in enumerate(zip(sources, targets))
    ]
    for copy in copies:
        copy.start()
    for copy in copies:
        copy.wait()


def body(
    availability,
    demand,
    gen_cost,
    cap_cost,
    owner_map,
    line_ends,
    line_limit,
    cross_ends,
    cross_limit,
    pair_counts,
    store_node,
    store_energy,
    store_power,
    price_start,
):
    rows, tech, nodes = availability.shape
    lines = line_limit.shape[0]
    units = store_node.shape[0]
    regions = lax.axis_size("region")
    hours = lax.axis_size("hours")
    size_a = 8 if hours % 64 == 0 else 2
    size_b = hours // size_a
    half = rows // 2
    slots = regions * LANES
    dma = pltpu.SemaphoreType.DMA
    arrays = (
        availability,
        demand,
        gen_cost,
        cap_cost,
        owner_map,
        line_ends,
        line_limit[None],
        cross_ends,
        cross_limit,
        pair_counts,
        store_node[None],
        store_energy[None],
        store_power[None],
        price_start,
    )
    scratch = [pltpu.VMEM(array.shape, array.dtype) for array in arrays] + [
        dma((len(arrays),)),
        pltpu.VMEM((rows, tech, nodes), F32),
        pltpu.VMEM((rows, tech, nodes), F32),
        pltpu.VMEM((rows, lines), F32),
        pltpu.VMEM((rows, units), F32),
        pltpu.VMEM((rows, units), F32),
        pltpu.VMEM((half, slots), F32),
        pltpu.VMEM((rows, nodes), F32),
        pltpu.VMEM((2 * nodes, slots), BF16),
        pltpu.VMEM((2 * nodes, slots), BF16),
        pltpu.VMEM((nodes, lines + units), BF16),
        pltpu.VMEM((1, slots), F32),
        pltpu.VMEM((1, slots), F32),
        pltpu.VMEM((1, slots), F32),
        pltpu.VMEM((regions, rows, nodes), F32),
        pltpu.VMEM((ITERS, regions, half, LANES), F32),
        pltpu.VMEM((ITERS, regions, half, LANES), F32),
        pltpu.VMEM((regions, 4, LANES), F32),
        pltpu.VMEM((regions, 4, LANES), F32),
        pltpu.VMEM((size_a, 2 * tech, nodes), F32),
        pltpu.VMEM((size_b, 2 * tech, nodes), F32),
        pltpu.VMEM((PHASES, size_a, tech, nodes), F32),
        pltpu.VMEM((PHASES, size_b, tech, nodes), F32),
        pltpu.VMEM((PHASES, hours // 2, 2, LANES), F32),
        pltpu.VMEM((PHASES, 2 * regions, 2, LANES), F32),
        pltpu.VMEM((PHASES, 2, 1, units), F32),
        pltpu.VMEM((PHASES, 2, 1, units), F32),
        pltpu.VMEM((1, LANES), F32),
        dma(()),
        dma(()),
        dma((ITERS,)),
        dma((ITERS,)),
        dma(()),
        dma(()),
        dma((2,)),
        dma((2,)),
        dma((PHASES, 2)),
        dma((PHASES, 2)),
        dma((PHASES, 2)),
        dma((PHASES, 2)),
        dma((PHASES, 2)),
        dma((PHASES, 2)),
    ]
    hbm = pl.BlockSpec(memory_space=pltpu.HBM)
    vmem = pl.BlockSpec(memory_space=pltpu.VMEM)
    outs = pl.pallas_call(
        functools.partial(kernel, (size_a // 2, size_b, regions)),
        out_shape=(
            pltpu.VMEM((rows, tech, nodes), F32),
            pltpu.VMEM(cap_cost.shape, F32),
            pltpu.VMEM((rows, nodes), F32),
            pltpu.VMEM((rows, units), F32),
        ),
        in_specs=[hbm] * len(arrays),
        out_specs=(vmem,) * 4,
        scratch_shapes=scratch,
        compiler_params=pltpu.CompilerParams(
            collective_id=0, has_side_effects=True, vmem_limit_bytes=60 * 1024 * 1024
        ),
    )(*arrays)
    return pl.pallas_call(
        store_outputs,
        out_shape=tuple(jax.ShapeDtypeStruct(out.shape, F32) for out in outs),
        in_specs=[vmem] * 4,
        out_specs=(hbm,) * 4,
        scratch_shapes=[dma((4,))],
        compiler_params=pltpu.CompilerParams(vmem_limit_bytes=4 * 1024 * 1024),
    )(*outs)


def solution(mesh):
    placed = (
        P("hours", None, "region"),
        P("hours", "region"),
        P(None, "region"),
        P("region", "hours"),
        P("region", None),
        P(None, "region"),
        P("region"),
        P(None, "region", None),
        P("region", None),
        P("region", None),
        P("region"),
        P("region"),
        P("region"),
        P("hours", "region"),
    )
    return jax.shard_map(
        body,
        mesh=mesh,
        in_specs=placed,
        out_specs=(
            P("hours", None, "region"),
            P("region", "hours"),
            P("hours", "region"),
            P("hours", "region"),
        ),
        check_vma=False,
    )
```
